32 devices in a mesh: facet: 4 (over y, core), sub: 8 (over z, x).
Axes of the slice: x: 2, y: 2, z: 4, core: 2. Of those that a mesh axis runs over, the one named last changes fastest.
Arguments:
- facet_data: bfloat16 [2, 16, 32768], P(None, None, ('facet', 'sub')), may hold values from -6 to 6
- subgrid_pos: int32 [32], P(('facet', 'sub')), may hold values from 0 to 32640, as said below
- vis_counts: int32 [32], P(('facet', 'sub')), may hold values from 128 to 512, as said below
- vis_u_fine: int32 [32, 512], P(('facet', 'sub')), may hold values from 0 to 8079
- vis_v_fine: int32 [32, 512], P(('facet', 'sub')), may hold values from 0 to 143
- vis_observed: float32 [2, 32, 512], P(None, ('facet', 'sub')), may hold values from -6 to 6
Outputs:
- vis_residual: float32 [2, 32, 512], P(None, ('facet', 'sub'))
- facet_residual: float32 [2, 16, 32768], P(None, None, ('facet', 'sub'))
The draws below stay inside these ranges and needn't reach their ends.
Inputs may be any that keep to these rules, and one draw needn't show every extreme that they name: `subgrid_pos`: distinct multiples of 128; a subgrid's u cells o to o + 511 are taken modulo 32768. The first vis_counts[s] slots of subgrid s are live; some subgrid has all 512 slots live.
All inputs are finite; a program needn't handle non-finite values.
Results may differ from the reference program's by a relative error of at most 0.012.
Values may be sent and summed in bfloat16 or wider, within the bound.
A program may use at most 64 MiB of HBM per device.

```python
import math
import jax
import jax.numpy as jnp
from jax import lax

SG = 512
KS = 8
OVER = 16
VR = 16
VIS = 512
NX = 32768
S_TOTAL = 32


def slot_product(left_side, right_side):
    right_high = right_side // 256
    right_low = right_side % 256
    return (left_side * right_low % NX + left_side * right_high % NX * 256) % NX


def special_spot(key):
    spot_count = 4 * NX // SG
    chosen_spot = jax.random.randint(jax.random.fold_in(key, 7), (), 5, spot_count - 5).astype(jnp.int32)
    below_cells = jax.random.randint(jax.random.fold_in(key, 8), (), SG // 16, 3 * SG // 16 + 1).astype(jnp.int32)
    return (chosen_spot, below_cells)


def draw_subgrid_pos(key, part):
    spot_count = 4 * NX // SG
    chosen_spot, below_cells = special_spot(key)
    spot_ids = jnp.arange(spot_count, dtype=jnp.int32)
    ranking = jax.random.permutation(jax.random.fold_in(key, 11), spot_count).astype(jnp.int32)
    excluded = (spot_ids == 0) | (spot_ids == spot_count - 1) | (spot_ids >= chosen_spot - 4) & (spot_ids <= chosen_spot)
    ranking = jnp.where(excluded, ranking + spot_count, ranking)
    ordered = jnp.argsort(ranking, stable=True).astype(jnp.int32)
    others = ordered[:S_TOTAL - 3]
    fixed_spots = jnp.stack([jnp.int32(0), jnp.int32(spot_count - 1), chosen_spot]).astype(jnp.int32)
    all_spots = jnp.concatenate([fixed_spots, others])
    shuffle = jax.random.permutation(jax.random.fold_in(key, 12), S_TOTAL)
    return (all_spots[shuffle] * (SG // 4)).astype(jnp.int32)


def draw_vis_counts(key, part):
    key_first, key_second = jax.random.split(key)
    counts = jax.random.randint(key_first, (S_TOTAL,), VIS // 4, VIS + 1).astype(jnp.int32)
    full_spot = jax.random.randint(key_second, (), 0, S_TOTAL)
    return counts.at[full_spot].set(VIS).astype(jnp.int32)


def draw_facet_data(key, part):
    chosen_spot, below_cells = special_spot(key)
    tone_cell = chosen_spot * (SG // 4) - below_cells
    column_ids = jnp.arange(NX, dtype=jnp.int32)
    tone_index = slot_product(column_ids, tone_cell)
    tone_angle = 2.0 * math.pi * (tone_index.astype(jnp.float32) / float(NX))
    row_angle = jax.random.uniform(jax.random.fold_in(key, 21), (VR, 1), jnp.float32, -math.pi, math.pi)
    total_angle = tone_angle[None, :] + row_angle
    tone_part = 4.0 * jnp.stack([jnp.cos(total_angle), jnp.sin(total_angle)])
    noise_part = 0.5 * jax.random.normal(jax.random.fold_in(key, 22), (2, VR, NX), jnp.float32)
    return jnp.clip(tone_part + noise_part, -6.0, 6.0).astype(jnp.bfloat16)


def place_ends(result, own_key, least, top_value):
    shape = result.shape
    spot = [jax.random.randint(jax.random.fold_in(own_key, axis), (), 0, shape[axis]) for axis in range(len(shape))]
    result = result.at[tuple(spot)].set(least)
    longest = shape.index(max(shape))
    spot[longest] = (spot[longest] + 1) % shape[longest]
    return result.at[tuple(spot)].set(top_value)


def level_of(stream_key, dims, cuts, least, largest):
    level = 1.0
    for axis_at, parts in cuts:
        draws = jax.random.uniform(jax.random.fold_in(jax.random.fold_in(stream_key, 6), axis_at), (parts,), jnp.float32, least / len(cuts), largest / len(cuts))
        level = level * jnp.repeat(jnp.exp(draws), dims[axis_at] // parts).reshape((-1,) + (1,) * (len(dims) - 1 - axis_at))
    return level


def noise(rng, dims, scale, reach, cuts=(), kind=jnp.bfloat16):
    values = jax.random.normal(rng, dims, jnp.float32) * scale
    if len(cuts) > 0:
        values = level_of(rng, dims, cuts, -0.22, 0.18) * values
    return jnp.clip(values, min=-reach, max=reach).astype(kind)


def setup_inputs(seed: int = 0) -> dict:
    key_of = jax.random.split(jax.random.key(seed), 7)
    facet_data = draw_facet_data(jax.random.fold_in(key_of[6], 71), 0)
    subgrid_pos = draw_subgrid_pos(jax.random.fold_in(key_of[6], 71), 0)
    vis_counts = draw_vis_counts(jax.random.fold_in(key_of[6], 71), 0)
    vis_u_fine = place_ends(jax.random.randint(key_of[3], (S_TOTAL, VIS), 0, (SG - KS + 1) * OVER), jax.random.fold_in(key_of[3], 1), 0, ((SG - KS + 1) * OVER) - 1).astype(jnp.int32)
    vis_v_fine = place_ends(jax.random.randint(key_of[4], (S_TOTAL, VIS), 0, (VR - KS + 1) * OVER), jax.random.fold_in(key_of[4], 1), 0, ((VR - KS + 1) * OVER) - 1).astype(jnp.int32)
    vis_observed = noise(key_of[5], (2, S_TOTAL, VIS), 1.0, 6.0, ((1, 32),), jnp.float32)
    return {"facet_data": facet_data, "subgrid_pos": subgrid_pos, "vis_counts": vis_counts, "vis_u_fine": vis_u_fine, "vis_v_fine": vis_v_fine, "vis_observed": vis_observed}


def phase_slot_index(left_side, right_side, image_width):
    right_high = right_side // 256
    right_low = right_side % 256
    return (left_side * right_low % image_width + left_side * right_high % image_width * 256) % image_width

def phasor(phase_total_count, image_width):
    phase_angle = 2.0 * math.pi * (phase_total_count.astype(jnp.float32) / float(image_width))
    return (jnp.cos(phase_angle), jnp.sin(phase_angle))

def build_phase_tables(sub_width, image_width):
    table_range = jnp.arange(sub_width, dtype=jnp.int32)
    cosine, sine_part = phasor(phase_slot_index(table_range[:, None], table_range[None, :], image_width), image_width)
    norm_scale = 1.0 / math.sqrt(image_width)
    real_part = (cosine * norm_scale).astype(jnp.bfloat16)
    imag_part = (-sine_part * norm_scale).astype(jnp.bfloat16)
    forward_table = jnp.concatenate([jnp.concatenate([real_part, imag_part], 1), jnp.concatenate([-imag_part, real_part], 1)], 0)
    backward_table = jnp.concatenate([jnp.concatenate([real_part, -imag_part], 1), jnp.concatenate([imag_part, real_part], 1)], 0)
    return (forward_table, backward_table)

def forward_part(columns, x_start, positions, table, image_width):
    sub_width = table.shape[0] // 2
    rows_v = columns.shape[1]
    blocks = columns.shape[2] // sub_width
    inside = jnp.arange(sub_width, dtype=jnp.int32)
    mod_cos, mod_sin = phasor(phase_slot_index(inside[None, :], positions[:, None], image_width), image_width)
    mod_cos = mod_cos[:, None, None, :]
    mod_sin = mod_sin[:, None, None, :]
    image_band = columns.astype(jnp.float32).reshape(2, rows_v, blocks, sub_width)
    real_z = image_band[0][None] * mod_cos + image_band[1][None] * mod_sin
    imag_z = image_band[1][None] * mod_cos - image_band[0][None] * mod_sin
    stacked = jnp.concatenate([real_z, imag_z], -1).astype(jnp.bfloat16)
    partial_grid = jnp.dot(stacked.astype(jnp.float32), table.astype(jnp.float32), precision=lax.Precision.HIGHEST)
    anchors = x_start + jnp.arange(blocks, dtype=jnp.int32) * sub_width
    columns_u = (positions[:, None] + inside[None, :]) % image_width
    post_cos, post_sin = phasor(phase_slot_index(anchors[None, :, None], columns_u[:, None, :], image_width), image_width)
    post_cos = post_cos[:, None]
    post_sin = post_sin[:, None]
    real_p = partial_grid[..., :sub_width]
    imag_p = partial_grid[..., sub_width:]
    real_g = lax.optimization_barrier(jnp.sum(real_p * post_cos + imag_p * post_sin, axis=2))
    imag_g = lax.optimization_barrier(jnp.sum(imag_p * post_cos - real_p * post_sin, axis=2))
    return jnp.concatenate([real_g, imag_g], -1)

def kernel_weights(fine_index, cells):
    cell_index = fine_index // OVER
    frac_index = fine_index % OVER
    cell_range = jnp.arange(cells, dtype=jnp.int32)
    cell_offset = cell_range[None, None, :] - cell_index[..., None]
    distance = cell_offset.astype(jnp.float32) - (KS - 1) / 2.0 - frac_index.astype(jnp.float32)[..., None] / OVER
    weight = jnp.exp(-0.5 * (distance / 0.6) ** 2)
    return jnp.where((cell_offset >= 0) & (cell_offset < KS), weight, jnp.float32(0.0))

def degrid_regrid(subgrid_data, u_fine, v_fine, counts, observed):
    sub_width = subgrid_data.shape[2] // 2
    weight_u = kernel_weights(u_fine, sub_width)
    kernel_weight_v = kernel_weights(v_fine, subgrid_data.shape[1])
    gridded_values = subgrid_data.astype(jnp.float32)
    along_v_axis = jnp.einsum('jtz,jzh->jth', kernel_weight_v, gridded_values, precision=lax.Precision.HIGHEST)
    real_pred = lax.optimization_barrier(jnp.sum(along_v_axis[..., :sub_width] * weight_u, -1))
    imag_pred = lax.optimization_barrier(jnp.sum(along_v_axis[..., sub_width:] * weight_u, -1))
    slot_range = jnp.arange(u_fine.shape[1], dtype=jnp.int32)
    live_mask = slot_range[None, :] < counts[:, None]
    real_res = jnp.where(live_mask, observed[0] - real_pred, jnp.float32(0.0))
    imag_res = jnp.where(live_mask, observed[1] - imag_pred, jnp.float32(0.0))
    spread_onto_grid = jnp.concatenate([real_res[..., None] * weight_u, imag_res[..., None] * weight_u], -1)
    regridded_values = jnp.einsum('mlz,mlr->mzr', kernel_weight_v, spread_onto_grid, precision=lax.Precision.HIGHEST).astype(jnp.bfloat16)
    return (jnp.stack([real_res, imag_res]), regridded_values)

def backward_part(grids, positions, x_start, span, table, image_width):
    sub_width = table.shape[0] // 2
    rows_v = grids.shape[1]
    blocks = span // sub_width
    inside = jnp.arange(sub_width, dtype=jnp.int32)
    anchors = x_start + jnp.arange(blocks, dtype=jnp.int32) * sub_width
    columns_u = (positions[:, None] + inside[None, :]) % image_width
    pre_cos, pre_sin = phasor(phase_slot_index(anchors[None, :, None], columns_u[:, None, :], image_width), image_width)
    pre_cos = pre_cos[:, None]
    pre_sin = pre_sin[:, None]
    real_h = grids[..., :sub_width].astype(jnp.float32)[:, :, None, :]
    imag_h = grids[..., sub_width:].astype(jnp.float32)[:, :, None, :]
    real_m = real_h * pre_cos - imag_h * pre_sin
    imag_m = real_h * pre_sin + imag_h * pre_cos
    stacked = jnp.concatenate([real_m, imag_m], -1).astype(jnp.bfloat16)
    product = jnp.dot(stacked.astype(jnp.float32), table.astype(jnp.float32), precision=lax.Precision.HIGHEST)
    mod_cos, mod_sin = phasor(phase_slot_index(inside[None, :], positions[:, None], image_width), image_width)
    mod_cos = mod_cos[:, None, None, :]
    mod_sin = mod_sin[:, None, None, :]
    real_q = product[..., :sub_width]
    imag_q = product[..., sub_width:]
    real_out = lax.optimization_barrier(jnp.sum(real_q * mod_cos - imag_q * mod_sin, axis=0))
    imag_out = lax.optimization_barrier(jnp.sum(real_q * mod_sin + imag_q * mod_cos, axis=0))
    return jnp.stack([real_out, imag_out]).reshape(2, rows_v, span)

def reference(facet_data, subgrid_pos, vis_counts, vis_u_fine, vis_v_fine, vis_observed):
    image_width = NX
    forward_table, backward_table = build_phase_tables(SG, image_width)
    observed = jnp.moveaxis(vis_observed, 1, 0)

    def one_subgrid(carried, sub_items):
        position, amount, u_fine, v_fine, seen_vis = sub_items
        subgrid_data = forward_part(facet_data, 0, position[None], forward_table, image_width).astype(jnp.bfloat16)
        residual, regridded_values = degrid_regrid(subgrid_data, u_fine[None], v_fine[None], amount[None], seen_vis[:, None])
        carried = carried + backward_part(regridded_values, position[None], 0, image_width, backward_table, image_width)
        return (carried, residual[:, 0])
    zero_image = jnp.zeros((2, VR, NX), jnp.float32)
    running, residuals = lax.scan(one_subgrid, zero_image, (subgrid_pos, vis_counts, vis_u_fine, vis_v_fine, observed))
    return (jnp.moveaxis(residuals, 0, 1), running)
```

```python
import functools
import math

import jax
import jax.numpy as jnp
import numpy as np
from jax import lax
from jax.experimental import pallas as pl
from jax.experimental.pallas import tpu as pltpu
from jax.sharding import PartitionSpec as P

SG = 512
KS = 8
OVER = 16
MESH = pl.DeviceIdType.MESH
F32 = jnp.float32
BF16 = jnp.bfloat16


class Plan:
    def __init__(self, devices, nsub, rows_v, columns):
        self.devices = devices
        self.nsub = nsub
        self.rows_v = rows_v
        self.width = columns * devices
        self.nb = self.width // SG
        self.rl = self.nb // devices
        self.times = SG // self.nb
        self.vg = min(rows_v, devices // 4)
        self.xg = devices // self.vg
        self.v2 = rows_v // self.vg
        self.xl = SG // self.xg
        self.used = self.rl * self.v2
        self.q = self.vg * 8
        self.x = self.xg * 128
        self.extra = 2 * self.xg


def block_transform(plan):
    ids = np.arange(plan.nb)
    angle = 2.0 * np.pi * ((ids[:, None] * ids[None, :]) % plan.nb) / plan.nb
    cosine = np.cos(angle).reshape(plan.devices, plan.rl, plan.devices, plan.rl)
    sine = np.sin(angle).reshape(plan.devices, plan.rl, plan.devices, plan.rl)
    table = np.zeros((plan.devices, 2, 4, plan.devices, 2, 4), np.float32)
    for i in range(plan.rl):
        for k in range(plan.rl):
            for v in range(plan.v2):
                out, into = i * plan.v2 + v, k * plan.v2 + v
                table[:, 0, out, :, 0, into] = cosine[:, i, :, k]
                table[:, 0, out, :, 1, into] = sine[:, i, :, k]
                table[:, 1, out, :, 0, into] = -sine[:, i, :, k]
                table[:, 1, out, :, 1, into] = cosine[:, i, :, k]
    return table.reshape(plan.devices * 8, plan.devices * 8)


def turn_table(plan):
    lane = np.arange(plan.x)
    x = (lane // 128) * plan.xl + lane % 128
    angle = 2.0 * np.pi * ((np.arange(8)[:, None] * x[None, :]) % SG) / SG
    return np.cos(angle).astype(np.float32), np.sin(angle).astype(np.float32)


def nt(a, b):
    return lax.dot_general(a, b, (((1,), (1,)), ((), ())), preferred_element_type=F32)


def tn(a, b):
    return lax.dot_general(a, b, (((0,), (0,)), ((), ())), preferred_element_type=F32)


def split(a):
    high = a.astype(BF16)
    return high, (a - high.astype(F32)).astype(BF16)


def swapped(a):
    row = lax.broadcasted_iota(jnp.int32, a.shape, 1)
    turned = pltpu.roll(a, 4, 1)
    return jnp.where(row < 4, turned, -turned)


def kernel(
    plan, prep, u_fine, v_fine, observed, count, high, low, back, turn_c, turn_s,
    res_out, image_out,
    r_a, s_b, r_b, s_c, r_c, s_d, r_d, s_e, r_e, s_f, r_f,
    wu, tch, tcl, tsh, tsl, send_sem, recv_sem,
):
    devices, nsub = plan.devices, plan.nsub
    me = lax.axis_index("facet") * nsub + lax.axis_index("sub")

    def place(i):
        target = lax.rem(me + i, devices)
        return target, (target // nsub, lax.rem(target, nsub))

    barrier = pltpu.get_barrier_semaphore()

    def greet(i, carry):
        pl.semaphore_signal(barrier, inc=1, device_id=place(i)[1], device_id_type=MESH)
        return carry

    lax.fori_loop(1, devices, greet, 0)
    pl.semaphore_wait(barrier, devices - 1)

    def send(phase, source, target):
        def one(i, carry):
            to, device = place(i)
            pltpu.make_async_remote_copy(
                src_ref=source.at[to],
                dst_ref=target.at[me],
                send_sem=send_sem.at[phase],
                recv_sem=recv_sem.at[phase],
                device_id=device,
                device_id_type=MESH,
            ).start()
            return carry

        lax.fori_loop(1, devices, one, 0)
        target[me] = source[me]

    def wait(sem, phase, target):
        others = target.at[pl.ds(0, devices - 1)]
        pltpu.make_async_copy(others, others, sem.at[phase]).wait()

    send(0, prep, r_a)

    cu = u_fine[...] // OVER
    shift = (KS - 1) / 2.0 + (u_fine[...] % OVER).astype(F32) / OVER
    half = devices * 8
    for i in range(plan.rl):
        row = lax.broadcasted_iota(jnp.int32, (half, u_fine.shape[1]), 0)
        cell = plan.nb * (row % 8) + (row // 8) * plan.rl + i
        offset = cell - cu
        distance = (offset.astype(F32) - shift) / 0.6
        weight = jnp.exp(-0.5 * distance * distance)
        weight = jnp.where((offset >= 0) & (offset < KS), weight, 0.0)
        wu[pl.ds(i * half, half), :] = weight.astype(BF16)

    shape = (plan.q, v_fine.shape[1])
    row = lax.broadcasted_iota(jnp.int32, shape, 0)
    offset = (row // 8) * plan.v2 + (row % 4) % plan.v2 - v_fine[...] // OVER
    shift = (KS - 1) / 2.0 + (v_fine[...] % OVER).astype(F32) / OVER
    distance = (offset.astype(F32) - shift) / 0.6
    wv = jnp.exp(-0.5 * distance * distance)
    wv = jnp.where((offset >= 0) & (offset < KS), wv, 0.0)

    row = lax.broadcasted_iota(jnp.int32, (8, plan.x), 0)
    lane = lax.broadcasted_iota(jnp.int32, (8, plan.x), 1)
    x = (lane // 128) * plan.xl + lane % 128
    r = me * plan.rl + (row % 4) // plan.v2
    angle = (2.0 * math.pi / plan.width) * ((x * r) % plan.width).astype(F32)
    scale = 1.0 / math.sqrt(plan.width)
    tw_c = (jnp.cos(angle) * scale)[None]
    tw_s = (jnp.sin(angle) * scale)[None]

    wait(recv_sem, 0, r_a)

    data = r_a[:, 0:8, :].reshape(half, 128).astype(BF16)
    total = jnp.dot(high[...], data, preferred_element_type=F32)
    total += jnp.dot(low[...], data, preferred_element_type=F32)
    s_b[...] = total.reshape(devices, 8, 128)
    send(1, s_b, r_b)

    for g in range(plan.xg):
        lanes = pl.ds(g * 128, 128)
        base_c = r_a[:, 8 + g : 9 + g, :]
        base_s = r_a[:, 8 + plan.xg + g : 9 + plan.xg + g, :]
        tc = base_c * turn_c[:, lanes][None] - base_s * turn_s[:, lanes][None]
        ts = base_s * turn_c[:, lanes][None] + base_c * turn_s[:, lanes][None]
        tch[:, lanes], tcl[:, lanes] = split(tc.reshape(half, 128))
        tsh[:, lanes], tsl[:, lanes] = split(ts.reshape(half, 128))

    wait(recv_sem, 1, r_b)

    got = r_b[...].reshape(plan.vg, plan.xg, 8, 128)
    a = jnp.concatenate([got[:, g] for g in range(plan.xg)], axis=2)
    a = a * tw_c + swapped(a) * tw_s
    a_h, a_l = split(a.reshape(plan.q, plan.x))
    w_h, w_l = split(swapped(a).reshape(plan.q, plan.x))
    grid = nt(tch[...], a_h) + nt(tsh[...], w_h)
    grid += nt(tch[...], a_l) + nt(tsh[...], w_l)
    grid += nt(tcl[...], a_h) + nt(tsl[...], w_h)
    s_c[...] = grid.reshape(devices, 8, plan.q)
    send(2, s_c, r_c)
    wait(recv_sem, 2, r_c)

    cells = r_c[...].reshape(half, plan.q)
    column = lax.broadcasted_iota(jnp.int32, (half, plan.q), 1)
    residue = (column % 4) // plan.v2
    parts = [jnp.where(residue == i, cells, 0.0) for i in range(plan.rl)]
    cells = jnp.concatenate(parts, axis=0).astype(BF16)
    along = tn(cells, wu[...]) * wv
    along = jnp.sum(along.reshape(plan.vg, 8, -1), axis=0)
    live = lax.broadcasted_iota(jnp.int32, (1, shape[1]), 1) < count[...]
    real = jnp.where(live, observed[0:1, :] - jnp.sum(along[0:4], axis=0, keepdims=True), 0.0)
    imag = jnp.where(live, observed[1:2, :] - jnp.sum(along[4:8], axis=0, keepdims=True), 0.0)
    res_out[0:1, :] = real
    res_out[1:2, :] = imag
    row = lax.broadcasted_iota(jnp.int32, shape, 0)
    spread = (wv * jnp.where(row % 8 < 4, real, imag)).astype(BF16)
    both = nt(wu[...], spread)
    regrid = both[0:half]
    for i in range(1, plan.rl):
        regrid = jnp.where(residue == i, both[i * half : (i + 1) * half], regrid)
    s_d[...] = regrid.astype(BF16).astype(F32).reshape(devices, 8, plan.q)
    send(3, s_d, r_d)
    wait(recv_sem, 3, r_d)

    cells = r_d[...].reshape(half, plan.q).astype(BF16)
    first = tn(cells, tch[...]).reshape(plan.vg, 8, plan.x)
    second = tn(cells, tsh[...]).reshape(plan.vg, 8, plan.x)
    a = first - swapped(second)
    a = a * tw_c - swapped(a) * tw_s
    parts = [a[:, None, :, g * 128 : (g + 1) * 128] for g in range(plan.xg)]
    s_e[...] = jnp.concatenate(parts, axis=1).reshape(devices, 8, 128)
    send(4, s_e, r_e)
    wait(recv_sem, 4, r_e)

    data = r_e[...].reshape(half, 128).astype(BF16)
    total = jnp.dot(back[...], data, preferred_element_type=F32)
    s_f[...] = total.reshape(devices, 8, 128)
    send(5, s_f, r_f)
    wait(recv_sem, 5, r_f)
    image_out[...] = r_f[...]

    for phase, sent in enumerate((r_a, r_b, r_c, r_d, r_e, r_f)):
        wait(send_sem, phase, sent)


def shards(facet_data, subgrid_pos, vis_counts, vis_u_fine, vis_v_fine, vis_observed):
    nsub = lax.axis_size("sub")
    devices = lax.axis_size("facet") * nsub
    plan = Plan(devices, nsub, facet_data.shape[1], facet_data.shape[2])
    slots = vis_u_fine.shape[1]

    image = facet_data.astype(F32).reshape(2, plan.vg, plan.v2, plan.rl, plan.xg, plan.xl)
    image = image.transpose(1, 4, 0, 3, 2, 5).reshape(devices, 2, plan.used, plan.xl)
    image = jnp.pad(image, ((0, 0), (0, 0), (0, 4 - plan.used), (0, 128 - plan.xl)))
    x = jnp.arange(SG, dtype=jnp.int32)
    angle = (2.0 * math.pi / SG) * ((x * (subgrid_pos[0] // plan.nb)) % SG).astype(F32)
    base = jnp.stack([jnp.cos(angle), jnp.sin(angle)]).reshape(plan.extra, plan.xl)
    base = jnp.pad(base, ((0, 0), (0, 128 - plan.xl)))
    base = jnp.broadcast_to(base[None], (devices, plan.extra, 128))
    prep = jnp.concatenate([image.reshape(devices, 8, 128), base], axis=1)

    table = block_transform(plan)
    high = table.astype(BF16)
    low = (table - high.astype(np.float32)).astype(BF16)
    turn_c, turn_s = turn_table(plan)

    first = pltpu.VMEM((devices, 8 + plan.extra, 128), F32)
    tile = pltpu.VMEM((devices, 8, 128), F32)
    cell = pltpu.VMEM((devices, 8, plan.q), F32)
    turn = pltpu.VMEM((devices * 8, plan.x), BF16)
    residual, out = pl.pallas_call(
        functools.partial(kernel, plan),
        out_shape=(
            jax.ShapeDtypeStruct((2, slots), F32),
            jax.ShapeDtypeStruct((devices, 8, 128), F32),
        ),
        in_specs=[pl.BlockSpec(memory_space=pltpu.VMEM)] * 10,
        out_specs=(pl.BlockSpec(memory_space=pltpu.VMEM),) * 2,
        scratch_shapes=[
            first, tile, tile, cell, cell, cell, cell, tile, tile, tile, tile,
            pltpu.VMEM((plan.rl * devices * 8, slots), BF16),
            turn, turn, turn, turn,
            pltpu.SemaphoreType.DMA((6,)),
            pltpu.SemaphoreType.DMA((6,)),
        ],
        compiler_params=pltpu.CompilerParams(
            collective_id=0, has_side_effects=True, vmem_limit_bytes=48 * 1024 * 1024
        ),
    )(
        prep, vis_u_fine, vis_v_fine, vis_observed[:, 0], vis_counts.reshape(1, 1),
        jnp.asarray(high), jnp.asarray(low), jnp.asarray(high.T), turn_c, turn_s,
    )
    out = out.reshape(plan.vg, plan.xg, 2, 4, 128)[:, :, :, : plan.used, : plan.xl]
    out = out.reshape(plan.vg, plan.xg, 2, plan.rl, plan.v2, plan.xl)
    out = out.transpose(2, 0, 4, 3, 1, 5).reshape(facet_data.shape)
    return residual[:, None, :], out


def solution(mesh):
    return jax.shard_map(
        shards,
        mesh=mesh,
        in_specs=(
            P(None, None, ("facet", "sub")),
            P(("facet", "sub")),
            P(("facet", "sub")),
            P(("facet", "sub"), None),
            P(("facet", "sub"), None),
            P(None, ("facet", "sub"), None),
        ),
        out_specs=(P(None, ("facet", "sub"), None), P(None, None, ("facet", "sub"))),
        check_vma=False,
    )
```

```python
import functools
import math

import jax
import jax.numpy as jnp
import numpy as np
from jax import lax
from jax.experimental import pallas as pl
from jax.experimental.pallas import tpu as pltpu
from jax.sharding import PartitionSpec as P

SG = 512
KS = 8
OVER = 16
MESH = pl.DeviceIdType.MESH
F32 = jnp.float32
BF16 = jnp.bfloat16
COSINE = [(-1) ** k / math.factorial(2 * k) for k in range(9)]
SINE = [(-1) ** k / math.factorial(2 * k + 1) for k in range(8)]


class Plan:
    def __init__(self, devices, nsub, rows_v, columns):
        self.devices = devices
        self.nsub = nsub
        self.rows_v = rows_v
        self.width = columns * devices
        self.nb = self.width // SG
        self.rl = self.nb // devices
        self.times = SG // self.nb
        self.vg = min(rows_v, devices // 4)
        self.xg = devices // self.vg
        self.v2 = rows_v // self.vg
        self.xl = SG // self.xg
        self.used = self.rl * self.v2
        self.q = self.vg * 8
        self.x = self.xg * 128


def block_transform(plan):
    ids = np.arange(plan.nb)
    angle = 2.0 * np.pi * ((ids[:, None] * ids[None, :]) % plan.nb) / plan.nb
    cosine = np.cos(angle).reshape(plan.devices, plan.rl, plan.devices, plan.rl)
    sine = np.sin(angle).reshape(plan.devices, plan.rl, plan.devices, plan.rl)
    table = np.zeros((plan.devices, 2, 4, plan.devices, 2, 4), np.float32)
    for i in range(plan.rl):
        for k in range(plan.rl):
            for v in range(plan.v2):
                out, into = i * plan.v2 + v, k * plan.v2 + v
                table[:, 0, out, :, 0, into] = cosine[:, i, :, k]
                table[:, 0, out, :, 1, into] = sine[:, i, :, k]
                table[:, 1, out, :, 0, into] = -sine[:, i, :, k]
                table[:, 1, out, :, 1, into] = cosine[:, i, :, k]
    return table.reshape(plan.devices * 8, plan.devices * 8)


def nt(a, b):
    return lax.dot_general(a, b, (((1,), (1,)), ((), ())), preferred_element_type=F32)


def tn(a, b):
    return lax.dot_general(a, b, (((0,), (0,)), ((), ())), preferred_element_type=F32)


def split(a):
    high = a.astype(BF16)
    return high, (a - high.astype(F32)).astype(BF16)


def swapped(a):
    row = lax.broadcasted_iota(jnp.int32, a.shape, 1)
    turned = pltpu.roll(a, 4, 1)
    return jnp.where(row < 4, turned, -turned)


def circle(p):
    h = p.astype(F32) * (2.0 * math.pi / SG) - math.pi
    square = h * h
    cosine = jnp.full(h.shape, COSINE[-1], F32)
    for k in reversed(COSINE[:-1]):
        cosine = cosine * square + k
    sine = jnp.full(h.shape, SINE[-1], F32)
    for k in reversed(SINE[:-1]):
        sine = sine * square + k
    return -cosine, -sine * h


def kernel(
    plan, facet, position, u_fine, v_fine, observed, count, high, low, back,
    res_out, image_out,
    image, slots, s_a, r_a, s_p, r_p, s_b, r_b, s_c, r_c, s_d, r_d, s_e, r_e, s_f, r_f,
    wu, tch, tcl, tsh, tsl, send_sem, recv_sem,
):
    devices, nsub = plan.devices, plan.nsub
    me = lax.axis_index("facet") * nsub + lax.axis_index("sub")
    half = devices * 8

    def place(i):
        target = lax.rem(me + i, devices)
        return target, (target // nsub, lax.rem(target, nsub))

    barrier = pltpu.get_barrier_semaphore()

    def greet(i, carry):
        pl.semaphore_signal(barrier, inc=1, device_id=place(i)[1], device_id_type=MESH)
        return carry

    lax.fori_loop(1, devices, greet, 0)

    def send(phase, source, target, same=False):
        def one(i, carry):
            to, device = place(i)
            pltpu.make_async_remote_copy(
                src_ref=source if same else source.at[to],
                dst_ref=target.at[me],
                send_sem=send_sem.at[phase],
                recv_sem=recv_sem.at[phase],
                device_id=device,
                device_id_type=MESH,
            ).start()
            return carry

        lax.fori_loop(1, devices, one, 0)
        target[me] = source[...] if same else source[me]

    def wait(sem, phase, target):
        others = target.at[pl.ds(0, devices - 1)]
        pltpu.make_async_copy(others, others, sem.at[phase]).wait()

    tiles = facet.shape[2] // 128
    per = 128 // plan.xl
    for k in range(tiles):
        image[:, k] = facet[:, :, k * 128 : (k + 1) * 128].astype(F32)
    slots[...] = jnp.zeros_like(slots)
    lane = lax.broadcasted_iota(jnp.int32, (plan.vg, 128), 1)

    def rows(c, k, v, g):
        return pl.ds(g * 8 + c * 4 + k * plan.v2 + v, plan.vg, stride=plan.xg * 8)

    for c in range(2):
        for k in range(plan.rl):
            for v in range(plan.v2):
                for g in range(plan.xg):
                    tile = (k * SG + g * plan.xl) // 128
                    value = image[c, tile, pl.ds(v, plan.vg, stride=plan.v2), :]
                    if per > 1:
                        if g % per:
                            value = pltpu.roll(value, 128 - (g % per) * plan.xl, 1)
                        value = jnp.where(lane < plan.xl, value, 0.0)
                    slots[rows(c, k, v, g), :] = value
    s_a[...] = slots[...].reshape(devices, 8, 128).astype(BF16)
    s_p[...] = jnp.broadcast_to(position[...] // plan.nb, s_p.shape)

    pl.semaphore_wait(barrier, devices - 1)
    send(0, s_a, r_a)
    send(6, s_p, r_p, same=True)

    cu = u_fine[...] // OVER
    shift = (KS - 1) / 2.0 + (u_fine[...] % OVER).astype(F32) / OVER
    for i in range(plan.rl):
        row = lax.broadcasted_iota(jnp.int32, (half, u_fine.shape[1]), 0)
        cell = plan.nb * (row & 7) + (row >> 3) * plan.rl + i
        offset = cell - cu
        distance = (offset.astype(F32) - shift) / 0.6
        weight = jnp.exp(-0.5 * distance * distance)
        weight = jnp.where((offset >= 0) & (offset < KS), weight, 0.0)
        wu[pl.ds(i * half, half), :] = weight.astype(BF16)

    shape = (plan.q, v_fine.shape[1])
    row = lax.broadcasted_iota(jnp.int32, shape, 0)
    offset = (row >> 3) * plan.v2 + lax.rem(row & 3, plan.v2) - v_fine[...] // OVER
    shift = (KS - 1) / 2.0 + (v_fine[...] % OVER).astype(F32) / OVER
    distance = (offset.astype(F32) - shift) / 0.6
    wv = jnp.exp(-0.5 * distance * distance)
    wv = jnp.where((offset >= 0) & (offset < KS), wv, 0.0)

    row = lax.broadcasted_iota(jnp.int32, (8, plan.x), 0)
    lane8 = lax.broadcasted_iota(jnp.int32, (8, plan.x), 1)
    x = (lane8 >> 7) * plan.xl + (lane8 & 127)
    r = me * plan.rl + lax.div(row & 3, plan.v2)
    angle = (2.0 * math.pi / plan.width) * lax.rem(x * r, plan.width).astype(F32)
    scale = 1.0 / math.sqrt(plan.width)
    tw_c = (jnp.cos(angle) * scale)[None]
    tw_s = (jnp.sin(angle) * scale)[None]

    wait(recv_sem, 0, r_a)

    data = r_a[...].astype(F32).reshape(half, 128).astype(BF16)
    total = jnp.dot(high[...], data, preferred_element_type=F32)
    total += jnp.dot(low[...], data, preferred_element_type=F32)
    s_b[...] = total.reshape(devices, 8, 128)
    send(1, s_b, r_b)

    wait(recv_sem, 6, r_p)
    cell = (devices, 8, 128)
    m = r_p[...] + lax.broadcasted_iota(jnp.int32, cell, 1)
    in_tile = lax.broadcasted_iota(jnp.int32, cell, 2)
    for g in range(plan.xg):
        lanes = pl.ds(g * 128, 128)
        tc, ts = circle((m * (in_tile + g * plan.xl)) & (SG - 1))
        tch[:, lanes], tcl[:, lanes] = split(tc.reshape(half, 128))
        tsh[:, lanes], tsl[:, lanes] = split(ts.reshape(half, 128))

    wait(recv_sem, 1, r_b)

    got = r_b[...].reshape(plan.vg, plan.xg, 8, 128)
    a = jnp.concatenate([got[:, g] for g in range(plan.xg)], axis=2)
    a = a * tw_c + swapped(a) * tw_s
    a_h, a_l = split(a.reshape(plan.q, plan.x))
    w_h, w_l = split(swapped(a).reshape(plan.q, plan.x))
    grid = nt(tch[...], jnp.concatenate([a_h, a_l], axis=0))
    grid += nt(tsh[...], jnp.concatenate([w_h, w_l], axis=0))
    grid = grid[:, : plan.q] + grid[:, plan.q :]
    grid += nt(tcl[...], a_h) + nt(tsl[...], w_h)
    s_c[...] = grid.reshape(devices, 8, plan.q).astype(BF16)
    send(2, s_c, r_c)
    wait(recv_sem, 2, r_c)

    cells = r_c[...].astype(F32).reshape(half, plan.q)
    column = lax.broadcasted_iota(jnp.int32, (half, plan.q), 1)
    residue = lax.div(column & 3, plan.v2)
    parts = [jnp.where(residue == i, cells, 0.0) for i in range(plan.rl)]
    cells = jnp.concatenate(parts, axis=0).astype(BF16)
    along = tn(cells, wu[...]) * wv
    along = jnp.sum(along.reshape(plan.vg, 8, -1), axis=0)
    live = lax.broadcasted_iota(jnp.int32, (1, shape[1]), 1) < count[...]
    real = jnp.where(live, observed[0] - jnp.sum(along[0:4], axis=0, keepdims=True), 0.0)
    imag = jnp.where(live, observed[1] - jnp.sum(along[4:8], axis=0, keepdims=True), 0.0)
    res_out[0] = real
    res_out[1] = imag
    row = lax.broadcasted_iota(jnp.int32, shape, 0)
    spread = (wv * jnp.where((row & 7) < 4, real, imag)).astype(BF16)
    both = nt(wu[...], spread)
    regrid = both[0:half]
    for i in range(1, plan.rl):
        regrid = jnp.where(residue == i, both[i * half : (i + 1) * half], regrid)
    s_d[...] = regrid.reshape(devices, 8, plan.q).astype(BF16)
    send(3, s_d, r_d)
    wait(recv_sem, 3, r_d)

    cells = r_d[...].astype(F32).reshape(half, plan.q).astype(BF16)
    first = tn(cells, tch[...]).reshape(plan.vg, 8, plan.x)
    second = tn(cells, tsh[...]).reshape(plan.vg, 8, plan.x)
    a = first - swapped(second)
    a = a * tw_c - swapped(a) * tw_s
    parts = [a[:, None, :, g * 128 : (g + 1) * 128] for g in range(plan.xg)]
    s_e[...] = jnp.concatenate(parts, axis=1).reshape(devices, 8, 128).astype(BF16)
    send(4, s_e, r_e)
    wait(recv_sem, 4, r_e)

    data = r_e[...].astype(F32).reshape(half, 128).astype(BF16)
    total = jnp.dot(back[...], data, preferred_element_type=F32)
    s_f[...] = total.reshape(devices, 8, 128).astype(BF16)
    send(5, s_f, r_f)
    wait(recv_sem, 5, r_f)

    slots[...] = r_f[...].astype(F32).reshape(half, 128)
    for c in range(2):
        for k in range(plan.rl):
            for v in range(plan.v2):
                for g in range(0, plan.xg, per):
                    value = slots[rows(c, k, v, g), :]
                    for n in range(1, per):
                        more = pltpu.roll(slots[rows(c, k, v, g + n), :], n * plan.xl, 1)
                        value = jnp.where(lane < n * plan.xl, value, more)
                    tile = (k * SG + g * plan.xl) // 128
                    image[c, tile, pl.ds(v, plan.vg, stride=plan.v2), :] = value
    for k in range(tiles):
        image_out[:, :, k * 128 : (k + 1) * 128] = image[:, k]

    for phase, sent in enumerate((r_a, r_b, r_c, r_d, r_e, r_f, r_p)):
        wait(send_sem, phase, sent)


def shards(facet_data, subgrid_pos, vis_counts, vis_u_fine, vis_v_fine, vis_observed):
    nsub = lax.axis_size("sub")
    devices = lax.axis_size("facet") * nsub
    plan = Plan(devices, nsub, facet_data.shape[1], facet_data.shape[2])
    slots = vis_u_fine.shape[1]

    table = block_transform(plan)
    high = table.astype(BF16)
    low = (table - high.astype(np.float32)).astype(BF16)

    wide = pltpu.VMEM((devices, 8, 128), F32)
    tile = pltpu.VMEM((devices, 8, 128), BF16)
    cell = pltpu.VMEM((devices, 8, plan.q), BF16)
    turn = pltpu.VMEM((devices * 8, plan.x), BF16)
    rows_v, columns = facet_data.shape[1:]
    return pl.pallas_call(
        functools.partial(kernel, plan),
        out_shape=(
            jax.ShapeDtypeStruct(vis_observed.shape, F32),
            jax.ShapeDtypeStruct(facet_data.shape, F32),
        ),
        in_specs=[pl.BlockSpec(memory_space=pltpu.VMEM)] * 9,
        out_specs=(pl.BlockSpec(memory_space=pltpu.VMEM),) * 2,
        scratch_shapes=[
            pltpu.VMEM((2, columns // 128, rows_v, 128), F32),
            pltpu.VMEM((devices * 8, 128), F32),
            tile, tile,
            pltpu.VMEM((1, 128), jnp.int32),
            pltpu.VMEM((devices, 1, 128), jnp.int32),
            wide, wide, cell, cell, cell, cell, tile, tile, tile, tile,
            pltpu.VMEM((plan.rl * devices * 8, slots), BF16),
            turn, turn, turn, turn,
            pltpu.SemaphoreType.DMA((7,)),
            pltpu.SemaphoreType.DMA((7,)),
        ],
        compiler_params=pltpu.CompilerParams(
            collective_id=0, has_side_effects=True, vmem_limit_bytes=48 * 1024 * 1024
        ),
    )(
        facet_data, subgrid_pos.reshape(1, 1), vis_u_fine, vis_v_fine, vis_observed,
        vis_counts.reshape(1, 1), jnp.asarray(high), jnp.asarray(low), jnp.asarray(high.T),
    )


def solution(mesh):
    return jax.shard_map(
        shards,
        mesh=mesh,
        in_specs=(
            P(None, None, ("facet", "sub")),
            P(("facet", "sub")),
            P(("facet", "sub")),
            P(("facet", "sub"), None),
            P(("facet", "sub"), None),
            P(None, ("facet", "sub"), None),
        ),
        out_specs=(P(None, ("facet", "sub"), None), P(None, None, ("facet", "sub"))),
        check_vma=False,
    )
```

```python
import functools
import math

import jax
import jax.numpy as jnp
import numpy as np
from jax import lax
from jax.experimental import pallas as pl
from jax.experimental.pallas import tpu as pltpu
from jax.sharding import PartitionSpec as P

SG = 512
KS = 8
OVER = 16
MESH = pl.DeviceIdType.MESH
F32 = jnp.float32
BF16 = jnp.bfloat16
COSINE = [(-1) ** k / math.factorial(2 * k) for k in range(9)]
SINE = [(-1) ** k / math.factorial(2 * k + 1) for k in range(8)]


class Plan:
    def __init__(self, devices, nsub, rows_v, columns):
        self.devices = devices
        self.nsub = nsub
        self.rows_v = rows_v
        self.width = columns * devices
        self.nb = self.width // SG
        self.rl = self.nb // devices
        self.times = SG // self.nb
        self.vg = min(rows_v, devices // 4)
        self.xg = devices // self.vg
        self.v2 = rows_v // self.vg
        self.xl = SG // self.xg
        self.used = self.rl * self.v2
        self.q = self.vg * 8
        self.x = self.xg * 128
        self.partners = sorted(range(1, devices), key=lambda i: -(i % nsub))


def block_transform(plan):
    ids = np.arange(plan.nb)
    angle = 2.0 * np.pi * ((ids[:, None] * ids[None, :]) % plan.nb) / plan.nb
    cosine = np.cos(angle).reshape(plan.devices, plan.rl, plan.devices, plan.rl)
    sine = np.sin(angle).reshape(plan.devices, plan.rl, plan.devices, plan.rl)
    table = np.zeros((plan.devices, 2, 4, plan.devices, 2, 4), np.float32)
    for i in range(plan.rl):
        for k in range(plan.rl):
            for v in range(plan.v2):
                out, into = i * plan.v2 + v, k * plan.v2 + v
                table[:, 0, out, :, 0, into] = cosine[:, i, :, k]
                table[:, 0, out, :, 1, into] = sine[:, i, :, k]
                table[:, 1, out, :, 0, into] = -sine[:, i, :, k]
                table[:, 1, out, :, 1, into] = cosine[:, i, :, k]
    return table.reshape(plan.devices * 8, plan.devices * 8)


def nt(a, b):
    return lax.dot_general(a, b, (((1,), (1,)), ((), ())), preferred_element_type=F32)


def tn(a, b):
    return lax.dot_general(a, b, (((0,), (0,)), ((), ())), preferred_element_type=F32)


def split(a):
    high = a.astype(BF16)
    return high, (a - high.astype(F32)).astype(BF16)


def swapped(a):
    row = lax.broadcasted_iota(jnp.int32, a.shape, 1)
    turned = pltpu.roll(a, 4, 1)
    return jnp.where(row < 4, turned, -turned)


def circle(p):
    h = p.astype(F32) * (2.0 * math.pi / SG) - math.pi
    square = h * h
    cosine = jnp.full(h.shape, COSINE[-1], F32)
    for k in reversed(COSINE[:-1]):
        cosine = cosine * square + k
    sine = jnp.full(h.shape, SINE[-1], F32)
    for k in reversed(SINE[:-1]):
        sine = sine * square + k
    return -cosine, -sine * h


def kernel(plan, *refs):
    operands, (res_out, image_out) = refs[:9], refs[9:11]
    (
        image, slots, s_a, r_a, s_p, r_p, s_b, r_b, s_c, r_c, s_d, r_d, s_e, r_e, s_f, r_f,
        wu, tch, tcl, tsh, tsl, send_sem, recv_sem, load_sem,
    ) = refs[11:35]
    held = refs[35:]
    facet, position, u_fine, v_fine, observed, count, high, low, back = held
    devices, nsub = plan.devices, plan.nsub
    me = lax.axis_index("facet") * nsub + lax.axis_index("sub")
    half = devices * 8

    loads = [
        pltpu.make_async_copy(operand, own, load_sem.at[n])
        for n, (operand, own) in enumerate(zip(operands, held))
    ]
    for load in loads:
        load.start()

    def place(i):
        target = me ^ i
        return target, (target // nsub, lax.rem(target, nsub))

    barrier = pltpu.get_barrier_semaphore()
    for i in plan.partners:
        pl.semaphore_signal(barrier, inc=1, device_id=place(i)[1], device_id_type=MESH)

    def send(phase, source, target, same=False):
        for i in plan.partners:
            to, device = place(i)
            pltpu.make_async_remote_copy(
                src_ref=source if same else source.at[to],
                dst_ref=target.at[me],
                send_sem=send_sem.at[phase],
                recv_sem=recv_sem.at[phase],
                device_id=device,
                device_id_type=MESH,
            ).start()
        target[me] = source[...] if same else source[me]

    def wait(sem, phase, target):
        others = target.at[pl.ds(0, devices - 1)]
        pltpu.make_async_copy(others, others, sem.at[phase]).wait()

    loads[0].wait()
    loads[1].wait()
    tiles = facet.shape[2] // 128
    per = 128 // plan.xl
    for k in range(tiles):
        image[:, k] = facet[:, :, k * 128 : (k + 1) * 128].astype(F32)
    slots[...] = jnp.zeros_like(slots)
    lane = lax.broadcasted_iota(jnp.int32, (plan.vg, 128), 1)

    def rows(c, k, v, g):
        return pl.ds(g * 8 + c * 4 + k * plan.v2 + v, plan.vg, stride=plan.xg * 8)

    for c in range(2):
        for k in range(plan.rl):
            for v in range(plan.v2):
                for g in range(plan.xg):
                    tile = (k * SG + g * plan.xl) // 128
                    value = image[c, tile, pl.ds(v, plan.vg, stride=plan.v2), :]
                    if per > 1:
                        if g % per:
                            value = pltpu.roll(value, 128 - (g % per) * plan.xl, 1)
                        value = jnp.where(lane < plan.xl, value, 0.0)
                    slots[rows(c, k, v, g), :] = value
    s_a[...] = slots[...].reshape(devices, 8, 128).astype(BF16)
    s_p[...] = jnp.broadcast_to(position[...] // plan.nb, s_p.shape)

    pl.semaphore_wait(barrier, devices - 1)
    send(0, s_a, r_a)
    send(6, s_p, r_p, same=True)

    loads[2].wait()
    cu = u_fine[...] // OVER
    shift = (KS - 1) / 2.0 + (u_fine[...] % OVER).astype(F32) / OVER
    for i in range(plan.rl):
        row = lax.broadcasted_iota(jnp.int32, (half, u_fine.shape[1]), 0)
        cell = plan.nb * (row & 7) + (row >> 3) * plan.rl + i
        offset = cell - cu
        distance = (offset.astype(F32) - shift) / 0.6
        weight = jnp.exp(-0.5 * distance * distance)
        weight = jnp.where((offset >= 0) & (offset < KS), weight, 0.0)
        wu[pl.ds(i * half, half), :] = weight.astype(BF16)

    loads[3].wait()
    shape = (plan.q, v_fine.shape[1])
    row = lax.broadcasted_iota(jnp.int32, shape, 0)
    offset = (row >> 3) * plan.v2 + lax.rem(row & 3, plan.v2) - v_fine[...] // OVER
    shift = (KS - 1) / 2.0 + (v_fine[...] % OVER).astype(F32) / OVER
    distance = (offset.astype(F32) - shift) / 0.6
    wv = jnp.exp(-0.5 * distance * distance)
    wv = jnp.where((offset >= 0) & (offset < KS), wv, 0.0)

    row = lax.broadcasted_iota(jnp.int32, (8, plan.x), 0)
    lane8 = lax.broadcasted_iota(jnp.int32, (8, plan.x), 1)
    x = (lane8 >> 7) * plan.xl + (lane8 & 127)
    r = me * plan.rl + lax.div(row & 3, plan.v2)
    angle = (2.0 * math.pi / plan.width) * lax.rem(x * r, plan.width).astype(F32)
    scale = 1.0 / math.sqrt(plan.width)
    tw_c = (jnp.cos(angle) * scale)[None]
    tw_s = (jnp.sin(angle) * scale)[None]

    for load in loads[4:]:
        load.wait()
    wait(recv_sem, 0, r_a)

    data = r_a[...].astype(F32).reshape(half, 128).astype(BF16)
    total = jnp.dot(high[...], data, preferred_element_type=F32)
    total += jnp.dot(low[...], data, preferred_element_type=F32)
    s_b[...] = total.reshape(devices, 8, 128)
    send(1, s_b, r_b)

    wait(recv_sem, 6, r_p)
    cell = (devices, 8, 128)
    m = r_p[...] + lax.broadcasted_iota(jnp.int32, cell, 1)
    in_tile = lax.broadcasted_iota(jnp.int32, cell, 2)
    for g in range(plan.xg):
        lanes = pl.ds(g * 128, 128)
        tc, ts = circle((m * (in_tile + g * plan.xl)) & (SG - 1))
        tch[:, lanes], tcl[:, lanes] = split(tc.reshape(half, 128))
        tsh[:, lanes], tsl[:, lanes] = split(ts.reshape(half, 128))

    wait(recv_sem, 1, r_b)

    got = r_b[...].reshape(plan.vg, plan.xg, 8, 128)
    a = jnp.concatenate([got[:, g] for g in range(plan.xg)], axis=2)
    a = a * tw_c + swapped(a) * tw_s
    a_h, a_l = split(a.reshape(plan.q, plan.x))
    w_h, w_l = split(swapped(a).reshape(plan.q, plan.x))
    grid = nt(tch[...], jnp.concatenate([a_h, a_l], axis=0))
    grid += nt(tsh[...], jnp.concatenate([w_h, w_l], axis=0))
    grid = grid[:, : plan.q] + grid[:, plan.q :]
    grid += nt(tcl[...], a_h) + nt(tsl[...], w_h)
    s_c[...] = grid.reshape(devices, 8, plan.q).astype(BF16)
    send(2, s_c, r_c)
    wait(recv_sem, 2, r_c)

    cells = r_c[...].astype(F32).reshape(half, plan.q)
    column = lax.broadcasted_iota(jnp.int32, (half, plan.q), 1)
    residue = lax.div(column & 3, plan.v2)
    parts = [jnp.where(residue == i, cells, 0.0) for i in range(plan.rl)]
    cells = jnp.concatenate(parts, axis=0).astype(BF16)
    along = tn(cells, wu[...]) * wv
    along = jnp.sum(along.reshape(plan.vg, 8, -1), axis=0)
    live = lax.broadcasted_iota(jnp.int32, (1, shape[1]), 1) < count[...]
    real = jnp.where(live, observed[0] - jnp.sum(along[0:4], axis=0, keepdims=True), 0.0)
    imag = jnp.where(live, observed[1] - jnp.sum(along[4:8], axis=0, keepdims=True), 0.0)
    res_out[0] = real
    res_out[1] = imag
    row = lax.broadcasted_iota(jnp.int32, shape, 0)
    spread = (wv * jnp.where((row & 7) < 4, real, imag)).astype(BF16)
    both = nt(wu[...], spread)
    regrid = both[0:half]
    for i in range(1, plan.rl):
        regrid = jnp.where(residue == i, both[i * half : (i + 1) * half], regrid)
    s_d[...] = regrid.reshape(devices, 8, plan.q).astype(BF16)
    send(3, s_d, r_d)
    wait(recv_sem, 3, r_d)

    cells = r_d[...].astype(F32).reshape(half, plan.q).astype(BF16)
    first = tn(cells, tch[...]).reshape(plan.vg, 8, plan.x)
    second = tn(cells, tsh[...]).reshape(plan.vg, 8, plan.x)
    a = first - swapped(second)
    a = a * tw_c - swapped(a) * tw_s
    parts = [a[:, None, :, g * 128 : (g + 1) * 128] for g in range(plan.xg)]
    s_e[...] = jnp.concatenate(parts, axis=1).reshape(devices, 8, 128).astype(BF16)
    send(4, s_e, r_e)
    wait(recv_sem, 4, r_e)

    data = r_e[...].astype(F32).reshape(half, 128).astype(BF16)
    total = jnp.dot(back[...], data, preferred_element_type=F32)
    s_f[...] = total.reshape(devices, 8, 128).astype(BF16)
    send(5, s_f, r_f)
    wait(recv_sem, 5, r_f)

    slots[...] = r_f[...].astype(F32).reshape(half, 128)
    for c in range(2):
        for k in range(plan.rl):
            for v in range(plan.v2):
                for g in range(0, plan.xg, per):
                    value = slots[rows(c, k, v, g), :]
                    for n in range(1, per):
                        more = pltpu.roll(slots[rows(c, k, v, g + n), :], n * plan.xl, 1)
                        value = jnp.where(lane < n * plan.xl, value, more)
                    tile = (k * SG + g * plan.xl) // 128
                    image[c, tile, pl.ds(v, plan.vg, stride=plan.v2), :] = value
    for k in range(tiles):
        image_out[:, :, k * 128 : (k + 1) * 128] = image[:, k]

    for phase, sent in enumerate((r_a, r_b, r_c, r_d, r_e, r_f, r_p)):
        wait(send_sem, phase, sent)


def shards(facet_data, subgrid_pos, vis_counts, vis_u_fine, vis_v_fine, vis_observed):
    nsub = lax.axis_size("sub")
    devices = lax.axis_size("facet") * nsub
    plan = Plan(devices, nsub, facet_data.shape[1], facet_data.shape[2])
    slots = vis_u_fine.shape[1]

    table = block_transform(plan)
    high = table.astype(BF16)
    low = (table - high.astype(np.float32)).astype(BF16)

    wide = pltpu.VMEM((devices, 8, 128), F32)
    tile = pltpu.VMEM((devices, 8, 128), BF16)
    cell = pltpu.VMEM((devices, 8, plan.q), BF16)
    turn = pltpu.VMEM((devices * 8, plan.x), BF16)
    rows_v, columns = facet_data.shape[1:]
    operands = (
        facet_data, subgrid_pos.reshape(1, 1), vis_u_fine, vis_v_fine, vis_observed,
        vis_counts.reshape(1, 1), jnp.asarray(high), jnp.asarray(low), jnp.asarray(high.T),
    )
    return pl.pallas_call(
        functools.partial(kernel, plan),
        out_shape=(
            jax.ShapeDtypeStruct(vis_observed.shape, F32),
            jax.ShapeDtypeStruct(facet_data.shape, F32),
        ),
        in_specs=[pl.BlockSpec(memory_space=pltpu.HBM)] * 9,
        out_specs=(pl.BlockSpec(memory_space=pltpu.VMEM),) * 2,
        scratch_shapes=[
            pltpu.VMEM((2, columns // 128, rows_v, 128), F32),
            pltpu.VMEM((devices * 8, 128), F32),
            tile, tile,
            pltpu.VMEM((1, 128), jnp.int32),
            pltpu.VMEM((devices, 1, 128), jnp.int32),
            wide, wide, cell, cell, cell, cell, tile, tile, tile, tile,
            pltpu.VMEM((plan.rl * devices * 8, slots), BF16),
            turn, turn, turn, turn,
            pltpu.SemaphoreType.DMA((7,)),
            pltpu.SemaphoreType.DMA((7,)),
            pltpu.SemaphoreType.DMA((9,)),
        ]
        + [pltpu.VMEM(one.shape, one.dtype) for one in operands],
        compiler_params=pltpu.CompilerParams(
            collective_id=0, has_side_effects=True, vmem_limit_bytes=64 * 1024 * 1024 - 65536
        ),
    )(*operands)


def solution(mesh):
    return jax.shard_map(
        shards,
        mesh=mesh,
        in_specs=(
            P(None, None, ("facet", "sub")),
            P(("facet", "sub")),
            P(("facet", "sub")),
            P(("facet", "sub"), None),
            P(("facet", "sub"), None),
            P(None, ("facet", "sub"), None),
        ),
        out_specs=(P(None, ("facet", "sub"), None), P(None, None, ("facet", "sub"))),
        check_vma=False,
    )
```

```python
import functools
import math

import jax
import jax.numpy as jnp
import numpy as np
from jax import lax
from jax.experimental import pallas as pl
from jax.experimental.pallas import tpu as pltpu
from jax.sharding import PartitionSpec as P

SG = 512
KS = 8
OVER = 16
MESH = pl.DeviceIdType.MESH
F32 = jnp.float32
BF16 = jnp.bfloat16
COSINE = [(-1) ** k / math.factorial(2 * k) for k in range(9)]
SINE = [(-1) ** k / math.factorial(2 * k + 1) for k in range(8)]


class Plan:
    def __init__(self, devices, nsub, rows_v, columns):
        self.devices = devices
        self.nsub = nsub
        self.rows_v = rows_v
        self.width = columns * devices
        self.nb = self.width // SG
        self.rl = self.nb // devices
        self.times = SG // self.nb
        self.vg = min(rows_v, devices // 4)
        self.xg = devices // self.vg
        self.v2 = rows_v // self.vg
        self.xl = SG // self.xg
        self.used = self.rl * self.v2
        self.q = self.vg * 8
        self.x = self.xg * 128
        self.partners = sorted(range(1, devices), key=lambda i: -(i % nsub))


def block_transform(plan):
    ids = np.arange(plan.nb)
    angle = 2.0 * np.pi * ((ids[:, None] * ids[None, :]) % plan.nb) / plan.nb
    cosine = np.cos(angle).reshape(plan.devices, plan.rl, plan.devices, plan.rl)
    sine = np.sin(angle).reshape(plan.devices, plan.rl, plan.devices, plan.rl)
    table = np.zeros((plan.devices, 2, 4, plan.devices, 2, 4), np.float32)
    for i in range(plan.rl):
        for k in range(plan.rl):
            for v in range(plan.v2):
                out, into = i * plan.v2 + v, k * plan.v2 + v
                table[:, 0, out, :, 0, into] = cosine[:, i, :, k]
                table[:, 0, out, :, 1, into] = sine[:, i, :, k]
                table[:, 1, out, :, 0, into] = -sine[:, i, :, k]
                table[:, 1, out, :, 1, into] = cosine[:, i, :, k]
    return table.reshape(plan.devices * 8, plan.devices * 8)


def nt(a, b):
    return lax.dot_general(a, b, (((1,), (1,)), ((), ())), preferred_element_type=F32)


def tn(a, b):
    return lax.dot_general(a, b, (((0,), (0,)), ((), ())), preferred_element_type=F32)


def split(a):
    high = a.astype(BF16)
    return high, (a - high.astype(F32)).astype(BF16)


def swapped(a):
    row = lax.broadcasted_iota(jnp.int32, a.shape, 1)
    turned = pltpu.roll(a, 4, 1)
    return jnp.where(row < 4, turned, -turned)


def circle(p):
    h = p.astype(F32) * (2.0 * math.pi / SG) - math.pi
    square = h * h
    cosine = jnp.full(h.shape, COSINE[-1], F32)
    for k in reversed(COSINE[:-1]):
        cosine = cosine * square + k
    sine = jnp.full(h.shape, SINE[-1], F32)
    for k in reversed(SINE[:-1]):
        sine = sine * square + k
    return -cosine, -sine * h


def rows(plan, c, k, v, g):
    return pl.ds(g * 8 + c * 4 + k * plan.v2 + v, plan.vg, stride=plan.xg * 8)


def kernel(plan, *refs):
    operands, (res_out, r_f) = refs[:9], refs[9:11]
    (
        image, slots, s_a, r_a, s_p, r_p, s_b, r_b, s_c, r_c, s_d, r_d, s_e, r_e, s_f,
        res, wu, tch, tcl, tsh, tsl, send_sem, recv_sem, load_sem,
    ) = refs[11:35]
    held = refs[35:]
    facet, position, u_fine, v_fine, observed, count, high, low, back = held
    devices, nsub = plan.devices, plan.nsub
    me = lax.axis_index("facet") * nsub + lax.axis_index("sub")
    half = devices * 8

    loads = [
        pltpu.make_async_copy(operand, own, load_sem.at[n])
        for n, (operand, own) in enumerate(zip(operands, held))
    ]
    for load in loads:
        load.start()

    def place(i):
        target = me ^ i
        return target, (target // nsub, lax.rem(target, nsub))

    barrier = pltpu.get_barrier_semaphore()
    for i in plan.partners:
        pl.semaphore_signal(barrier, inc=1, device_id=place(i)[1], device_id_type=MESH)

    def send(phase, source, target, same=False, local=False):
        for i in plan.partners:
            to, device = place(i)
            pltpu.make_async_remote_copy(
                src_ref=source if same else source.at[to],
                dst_ref=target.at[me],
                send_sem=send_sem.at[phase],
                recv_sem=recv_sem.at[phase],
                device_id=device,
                device_id_type=MESH,
            ).start()
        if not local:
            target[me] = source[...] if same else source[me]

    def wait(sem, phase, target):
        others = target.at[pl.ds(0, devices - 1)]
        pltpu.make_async_copy(others, others, sem.at[phase]).wait()

    loads[0].wait()
    loads[1].wait()
    tiles = facet.shape[2] // 128
    per = 128 // plan.xl
    for k in range(tiles):
        image[:, k] = facet[:, :, k * 128 : (k + 1) * 128].astype(F32)
    slots[...] = jnp.zeros_like(slots)
    lane = lax.broadcasted_iota(jnp.int32, (plan.vg, 128), 1)

    for c in range(2):
        for k in range(plan.rl):
            for v in range(plan.v2):
                for g in range(plan.xg):
                    tile = (k * SG + g * plan.xl) // 128
                    value = image[c, tile, pl.ds(v, plan.vg, stride=plan.v2), :]
                    if per > 1:
                        if g % per:
                            value = pltpu.roll(value, 128 - (g % per) * plan.xl, 1)
                        value = jnp.where(lane < plan.xl, value, 0.0)
                    slots[rows(plan, c, k, v, g), :] = value
    s_a[...] = slots[...].reshape(devices, 8, 128).astype(BF16)
    s_p[...] = jnp.broadcast_to(position[...] // plan.nb, s_p.shape)

    pl.semaphore_wait(barrier, devices - 1)
    send(0, s_a, r_a)
    send(6, s_p, r_p, same=True)

    row = lax.broadcasted_iota(jnp.int32, (8, plan.x), 0)
    lane8 = lax.broadcasted_iota(jnp.int32, (8, plan.x), 1)
    x = (lane8 >> 7) * plan.xl + (lane8 & 127)
    r = me * plan.rl + lax.div(row & 3, plan.v2)
    angle = (2.0 * math.pi / plan.width) * lax.rem(x * r, plan.width).astype(F32)
    scale = 1.0 / math.sqrt(plan.width)
    tw_c = (jnp.cos(angle) * scale)[None]
    tw_s = (jnp.sin(angle) * scale)[None]

    for load in loads[2:]:
        load.wait()
    wait(recv_sem, 0, r_a)

    data = r_a[...].astype(F32).reshape(half, 128).astype(BF16)
    total = jnp.dot(high[...], data, preferred_element_type=F32)
    total += jnp.dot(low[...], data, preferred_element_type=F32)
    s_b[...] = total.reshape(devices, 8, 128)
    send(1, s_b, r_b)

    wait(recv_sem, 6, r_p)
    cell = (devices, 8, 128)
    m = r_p[...] + lax.broadcasted_iota(jnp.int32, cell, 1)
    in_tile = lax.broadcasted_iota(jnp.int32, cell, 2)
    for g in range(plan.xg):
        lanes = pl.ds(g * 128, 128)
        tc, ts = circle((m * (in_tile + g * plan.xl)) & (SG - 1))
        tch[:, lanes], tcl[:, lanes] = split(tc.reshape(half, 128))
        tsh[:, lanes], tsl[:, lanes] = split(ts.reshape(half, 128))

    wait(recv_sem, 1, r_b)

    got = r_b[...].reshape(plan.vg, plan.xg, 8, 128)
    a = jnp.concatenate([got[:, g] for g in range(plan.xg)], axis=2)
    a = a * tw_c + swapped(a) * tw_s
    a_h, a_l = split(a.reshape(plan.q, plan.x))
    w_h, w_l = split(swapped(a).reshape(plan.q, plan.x))
    grid = nt(tch[...], jnp.concatenate([a_h, a_l], axis=0))
    grid += nt(tsh[...], jnp.concatenate([w_h, w_l], axis=0))
    grid = grid[:, : plan.q] + grid[:, plan.q :]
    grid += nt(tcl[...], a_h) + nt(tsl[...], w_h)
    s_c[...] = grid.reshape(devices, 8, plan.q).astype(BF16)
    send(2, s_c, r_c)

    cu = u_fine[...] // OVER
    shift = (KS - 1) / 2.0 + (u_fine[...] % OVER).astype(F32) / OVER
    for i in range(plan.rl):
        row = lax.broadcasted_iota(jnp.int32, (half, u_fine.shape[1]), 0)
        cell = plan.nb * (row & 7) + (row >> 3) * plan.rl + i
        offset = cell - cu
        distance = (offset.astype(F32) - shift) / 0.6
        weight = jnp.exp(-0.5 * distance * distance)
        weight = jnp.where((offset >= 0) & (offset < KS), weight, 0.0)
        wu[pl.ds(i * half, half), :] = weight.astype(BF16)

    shape = (plan.q, v_fine.shape[1])
    row = lax.broadcasted_iota(jnp.int32, shape, 0)
    offset = (row >> 3) * plan.v2 + lax.rem(row & 3, plan.v2) - v_fine[...] // OVER
    shift = (KS - 1) / 2.0 + (v_fine[...] % OVER).astype(F32) / OVER
    distance = (offset.astype(F32) - shift) / 0.6
    wv = jnp.exp(-0.5 * distance * distance)
    wv = jnp.where((offset >= 0) & (offset < KS), wv, 0.0)

    wait(recv_sem, 2, r_c)

    cells = r_c[...].astype(F32).reshape(half, plan.q)
    column = lax.broadcasted_iota(jnp.int32, (half, plan.q), 1)
    residue = lax.div(column & 3, plan.v2)
    parts = [jnp.where(residue == i, cells, 0.0) for i in range(plan.rl)]
    cells = jnp.concatenate(parts, axis=0).astype(BF16)
    along = tn(cells, wu[...]) * wv
    along = jnp.sum(along.reshape(plan.vg, 8, -1), axis=0)
    live = lax.broadcasted_iota(jnp.int32, (1, shape[1]), 1) < count[...]
    real = jnp.where(live, observed[0] - jnp.sum(along[0:4], axis=0, keepdims=True), 0.0)
    imag = jnp.where(live, observed[1] - jnp.sum(along[4:8], axis=0, keepdims=True), 0.0)
    res[0] = real
    res[1] = imag
    kept = pltpu.make_async_copy(res, res_out, load_sem.at[0])
    kept.start()
    row = lax.broadcasted_iota(jnp.int32, shape, 0)
    spread = (wv * jnp.where((row & 7) < 4, real, imag)).astype(BF16)
    both = nt(wu[...], spread)
    regrid = both[0:half]
    for i in range(1, plan.rl):
        regrid = jnp.where(residue == i, both[i * half : (i + 1) * half], regrid)
    s_d[...] = regrid.reshape(devices, 8, plan.q).astype(BF16)
    send(3, s_d, r_d)
    wait(recv_sem, 3, r_d)

    cells = r_d[...].astype(F32).reshape(half, plan.q).astype(BF16)
    first = tn(cells, tch[...]).reshape(plan.vg, 8, plan.x)
    second = tn(cells, tsh[...]).reshape(plan.vg, 8, plan.x)
    a = first - swapped(second)
    a = a * tw_c - swapped(a) * tw_s
    parts = [a[:, None, :, g * 128 : (g + 1) * 128] for g in range(plan.xg)]
    s_e[...] = jnp.concatenate(parts, axis=1).reshape(devices, 8, 128).astype(BF16)
    send(4, s_e, r_e)
    wait(recv_sem, 4, r_e)

    data = r_e[...].astype(F32).reshape(half, 128).astype(BF16)
    total = jnp.dot(back[...], data, preferred_element_type=F32)
    s_f[...] = total.reshape(devices, 8, 128).astype(BF16)
    send(5, s_f, r_f, local=True)
    own = pltpu.make_async_copy(s_f.at[me], r_f.at[me], load_sem.at[1])
    own.start()
    wait(recv_sem, 5, r_f)
    own.wait()
    kept.wait()

    for phase, sent in enumerate((r_a, r_b, r_c, r_d, r_e, r_f, r_p)):
        wait(send_sem, phase, sent)


def finish(plan, residual, got, res_out, image_out, image, slots):
    res_out[...] = residual[...]
    tiles = image_out.shape[2] // 128
    per = 128 // plan.xl
    lane = lax.broadcasted_iota(jnp.int32, (plan.vg, 128), 1)
    slots[...] = got[...].astype(F32).reshape(plan.devices * 8, 128)
    for c in range(2):
        for k in range(plan.rl):
            for v in range(plan.v2):
                for g in range(0, plan.xg, per):
                    value = slots[rows(plan, c, k, v, g), :]
                    for n in range(1, per):
                        more = pltpu.roll(slots[rows(plan, c, k, v, g + n), :], n * plan.xl, 1)
                        value = jnp.where(lane < n * plan.xl, value, more)
                    tile = (k * SG + g * plan.xl) // 128
                    image[c, tile, pl.ds(v, plan.vg, stride=plan.v2), :] = value
    for k in range(tiles):
        image_out[:, :, k * 128 : (k + 1) * 128] = image[:, k]


def shards(facet_data, subgrid_pos, vis_counts, vis_u_fine, vis_v_fine, vis_observed):
    nsub = lax.axis_size("sub")
    devices = lax.axis_size("facet") * nsub
    plan = Plan(devices, nsub, facet_data.shape[1], facet_data.shape[2])
    slots = vis_u_fine.shape[1]

    table = block_transform(plan)
    high = table.astype(BF16)
    low = (table - high.astype(np.float32)).astype(BF16)

    wide = pltpu.VMEM((devices, 8, 128), F32)
    tile = pltpu.VMEM((devices, 8, 128), BF16)
    cell = pltpu.VMEM((devices, 8, plan.q), BF16)
    turn = pltpu.VMEM((devices * 8, plan.x), BF16)
    rows_v, columns = facet_data.shape[1:]
    operands = (
        facet_data, subgrid_pos.reshape(1, 1), vis_u_fine, vis_v_fine, vis_observed,
        vis_counts.reshape(1, 1), jnp.asarray(high), jnp.asarray(low), jnp.asarray(high.T),
    )
    residual, got = pl.pallas_call(
        functools.partial(kernel, plan),
        out_shape=(
            jax.ShapeDtypeStruct(vis_observed.shape, F32),
            jax.ShapeDtypeStruct((devices, 8, 128), BF16),
        ),
        in_specs=[pl.BlockSpec(memory_space=pltpu.HBM)] * 9,
        out_specs=(pl.BlockSpec(memory_space=pltpu.HBM),) * 2,
        scratch_shapes=[
            pltpu.VMEM((2, columns // 128, rows_v, 128), F32),
            pltpu.VMEM((devices * 8, 128), F32),
            tile, tile,
            pltpu.VMEM((1, 128), jnp.int32),
            pltpu.VMEM((devices, 1, 128), jnp.int32),
            wide, wide, cell, cell, cell, cell, tile, tile, tile,
            pltpu.VMEM(vis_observed.shape, F32),
            pltpu.VMEM((plan.rl * devices * 8, slots), BF16),
            turn, turn, turn, turn,
            pltpu.SemaphoreType.DMA((7,)),
            pltpu.SemaphoreType.DMA((7,)),
            pltpu.SemaphoreType.DMA((9,)),
        ]
        + [pltpu.VMEM(one.shape, one.dtype) for one in operands],
        compiler_params=pltpu.CompilerParams(
            collective_id=0, has_side_effects=True, vmem_limit_bytes=64 * 1024 * 1024 - 65536
        ),
    )(*operands)
    return pl.pallas_call(
        functools.partial(finish, plan),
        out_shape=(
            jax.ShapeDtypeStruct(vis_observed.shape, F32),
            jax.ShapeDtypeStruct(facet_data.shape, F32),
        ),
        in_specs=[pl.BlockSpec(memory_space=pltpu.VMEM)] * 2,
        out_specs=(pl.BlockSpec(memory_space=pltpu.VMEM),) * 2,
        scratch_shapes=[
            pltpu.VMEM((2, columns // 128, rows_v, 128), F32),
            pltpu.VMEM((devices * 8, 128), F32),
        ],
        compiler_params=pltpu.CompilerParams(vmem_limit_bytes=64 * 1024 * 1024 - 65536),
    )(residual, got)


def solution(mesh):
    return jax.shard_map(
        shards,
        mesh=mesh,
        in_specs=(
            P(None, None, ("facet", "sub")),
            P(("facet", "sub")),
            P(("facet", "sub")),
            P(("facet", "sub"), None),
            P(("facet", "sub"), None),
            P(None, ("facet", "sub"), None),
        ),
        out_specs=(P(None, ("facet", "sub"), None), P(None, None, ("facet", "sub"))),
        check_vma=False,
    )
```

```python
import functools
import math

import jax
import jax.numpy as jnp
import numpy as np
from jax import lax
from jax.experimental import pallas as pl
from jax.experimental.pallas import tpu as pltpu
from jax.sharding import PartitionSpec as P

SG = 512
KS = 8
OVER = 16
MESH = pl.DeviceIdType.MESH
F32 = jnp.float32
BF16 = jnp.bfloat16
COSINE = [(-1) ** k / math.factorial(2 * k) for k in range(9)]
SINE = [(-1) ** k / math.factorial(2 * k + 1) for k in range(8)]


class Plan:
    def __init__(self, devices, nsub, rows_v, columns):
        self.devices = devices
        self.nsub = nsub
        self.rows_v = rows_v
        self.width = columns * devices
        self.nb = self.width // SG
        self.rl = self.nb // devices
        self.vg = nsub
        self.xg = devices // nsub
        self.v2 = rows_v // self.vg
        self.xl = SG // self.xg
        self.res = self.nb // self.xg
        self.cv = 2 * self.v2
        self.q = self.cv * self.res
        self.x = self.xg * 128
        self.partners = sorted(range(1, devices), key=lambda i: -(i % nsub))


def block_transform(plan):
    ids = np.arange(plan.nb)
    angle = 2.0 * np.pi * ((ids[:, None] * ids[None, :]) % plan.nb) / plan.nb
    cosine = np.cos(angle).reshape(plan.xg, plan.res, plan.devices, plan.rl)
    sine = np.sin(angle).reshape(plan.xg, plan.res, plan.devices, plan.rl)
    table = np.zeros((plan.xg, 2, plan.v2, plan.res, plan.devices, 2, 4), np.float32)
    for k in range(plan.rl):
        for v in range(plan.v2):
            into = k * plan.v2 + v
            table[:, 0, v, :, :, 0, into] = cosine[..., k]
            table[:, 0, v, :, :, 1, into] = sine[..., k]
            table[:, 1, v, :, :, 0, into] = -sine[..., k]
            table[:, 1, v, :, :, 1, into] = cosine[..., k]
    return table.reshape(plan.xg * plan.q, plan.devices * 8)


def nt(a, b):
    return lax.dot_general(a, b, (((1,), (1,)), ((), ())), preferred_element_type=F32)


def tn(a, b):
    return lax.dot_general(a, b, (((0,), (0,)), ((), ())), preferred_element_type=F32)


def split(a):
    high = a.astype(BF16)
    return high, (a - high.astype(F32)).astype(BF16)


def swapped(a):
    middle = a.shape[0] // 2
    return jnp.concatenate([a[middle:], -a[:middle]], axis=0)


def circle(p, period):
    h = p.astype(F32) * (2.0 * math.pi / period) - math.pi
    square = h * h
    cosine = jnp.full(h.shape, COSINE[-1], F32)
    for k in reversed(COSINE[:-1]):
        cosine = cosine * square + k
    sine = jnp.full(h.shape, SINE[-1], F32)
    for k in reversed(SINE[:-1]):
        sine = sine * square + k
    return -cosine, -sine * h


def rows(plan, c, k, v, g):
    return pl.ds(g * plan.vg * 8 + c * 4 + k * plan.v2 + v, plan.vg, stride=8)


def kernel(plan, *refs):
    operands, (res_out, r_f) = refs[:9], refs[9:11]
    (
        image, slots, s_a, r_a, s_p, r_p, s_b, r_b, s_c, r_c, s_d, r_d, s_e, r_e, s_f,
        res, wu, tch, tcl, tsh, tsl, send_sem, recv_sem, load_sem,
    ) = refs[11:35]
    held = refs[35:]
    facet, position, u_fine, v_fine, observed, count, high, low, back = held
    devices, nsub = plan.devices, plan.nsub
    group, column = lax.axis_index("facet"), lax.axis_index("sub")
    me = group * nsub + column
    half = devices * 8

    loads = [
        pltpu.make_async_copy(operand, own, load_sem.at[n])
        for n, (operand, own) in enumerate(zip(operands, held))
    ]
    for load in loads:
        load.start()

    def place(i):
        target = me ^ i
        return target, (target // nsub, lax.rem(target, nsub))

    barrier = pltpu.get_barrier_semaphore()
    for i in plan.partners:
        pl.semaphore_signal(barrier, inc=1, device_id=place(i)[1], device_id_type=MESH)

    def send(phase, source, target, same=False, local=False):
        for i in plan.partners:
            to, device = place(i)
            pltpu.make_async_remote_copy(
                src_ref=source if same else source.at[to],
                dst_ref=target.at[me],
                send_sem=send_sem.at[phase],
                recv_sem=recv_sem.at[phase],
                device_id=device,
                device_id_type=MESH,
            ).start()
        if not local:
            target[me] = source[...] if same else source[me]

    def across(phase, source, target):
        for i in range(1, plan.xg):
            pltpu.make_async_remote_copy(
                src_ref=source.at[group ^ i],
                dst_ref=target.at[group],
                send_sem=send_sem.at[phase],
                recv_sem=recv_sem.at[phase],
                device_id=(group ^ i, column),
                device_id_type=MESH,
            ).start()
        target[group] = source[group]

    def wait(sem, phase, target):
        others = target.at[pl.ds(0, target.shape[0] - 1)]
        pltpu.make_async_copy(others, others, sem.at[phase]).wait()

    loads[0].wait()
    loads[1].wait()
    tiles = facet.shape[2] // 128
    per = 128 // plan.xl
    for k in range(tiles):
        image[:, k] = facet[:, :, k * 128 : (k + 1) * 128].astype(F32)
    slots[...] = jnp.zeros_like(slots)
    lane = lax.broadcasted_iota(jnp.int32, (plan.vg, 128), 1)

    for c in range(2):
        for k in range(plan.rl):
            for v in range(plan.v2):
                for g in range(plan.xg):
                    tile = (k * SG + g * plan.xl) // 128
                    value = image[c, tile, pl.ds(v, plan.vg, stride=plan.v2), :]
                    if per > 1:
                        if g % per:
                            value = pltpu.roll(value, 128 - (g % per) * plan.xl, 1)
                        value = jnp.where(lane < plan.xl, value, 0.0)
                    slots[rows(plan, c, k, v, g), :] = value
    s_a[...] = slots[...].reshape(devices, 8, 128).astype(BF16)
    s_p[...] = jnp.broadcast_to(position[...] // plan.nb, s_p.shape)

    pl.semaphore_wait(barrier, devices - 1)
    send(0, s_a, r_a)
    send(6, s_p, r_p, same=True)

    row = lax.broadcasted_iota(jnp.int32, (plan.res, plan.x), 0)
    lane8 = lax.broadcasted_iota(jnp.int32, (plan.res, plan.x), 1)
    x = (lane8 >> 7) * plan.xl + (lane8 & 127)
    tw_c, tw_s = circle((x * (group * plan.res + row)) & (plan.width - 1), plan.width)
    scale = 1.0 / math.sqrt(plan.width)
    tw_c = jnp.concatenate([tw_c * scale] * plan.cv, axis=0)
    tw_s = jnp.concatenate([tw_s * scale] * plan.cv, axis=0)

    for load in loads[2:]:
        load.wait()
    wait(recv_sem, 0, r_a)

    data = r_a[...].astype(F32).reshape(half, 128).astype(BF16)
    total = jnp.dot(high[...], data, preferred_element_type=F32)
    total += jnp.dot(low[...], data, preferred_element_type=F32)
    s_b[...] = total.reshape(plan.xg, plan.q, 128)
    across(1, s_b, r_b)

    wait(recv_sem, 6, r_p)
    cell = (devices, 8, 128)
    m = r_p[...] + lax.broadcasted_iota(jnp.int32, cell, 1)
    in_tile = lax.broadcasted_iota(jnp.int32, cell, 2)
    for g in range(plan.xg):
        lanes = pl.ds(g * 128, 128)
        tc, ts = circle((m * (in_tile + g * plan.xl)) & (SG - 1), SG)
        tch[:, lanes], tcl[:, lanes] = split(tc.reshape(half, 128))
        tsh[:, lanes], tsl[:, lanes] = split(ts.reshape(half, 128))

    wait(recv_sem, 1, r_b)

    a = jnp.concatenate([r_b[g] for g in range(plan.xg)], axis=1)
    a = a * tw_c + swapped(a) * tw_s
    a_h, a_l = split(a)
    w_h, w_l = split(swapped(a))
    grid = nt(tch[...], a_h) + nt(tsh[...], w_h)
    grid += nt(tch[...], a_l) + nt(tsh[...], w_l)
    grid += nt(tcl[...], a_h) + nt(tsl[...], w_h)
    s_c[...] = grid.reshape(devices, 8, plan.q).astype(BF16)
    send(2, s_c, r_c)

    cu = u_fine[...] // OVER
    shift = (KS - 1) / 2.0 + (u_fine[...] % OVER).astype(F32) / OVER
    part = plan.xg * plan.res
    for t in range(8):
        row = lax.broadcasted_iota(jnp.int32, (part, u_fine.shape[1]), 0)
        offset = row + plan.nb * t - cu
        distance = (offset.astype(F32) - shift) / 0.6
        weight = jnp.exp(-0.5 * distance * distance)
        weight = jnp.where((offset >= 0) & (offset < KS), weight, 0.0)
        wu[pl.ds(t * part, part), :] = weight.astype(BF16)

    span = plan.vg * 8
    shape = (plan.cv * span, v_fine.shape[1])
    row = lax.broadcasted_iota(jnp.int32, shape, 0)
    v = lax.rem(lax.div(row, span), plan.v2) + lax.div(lax.rem(row, span), 8) * plan.v2
    offset = v - v_fine[...] // OVER
    shift = (KS - 1) / 2.0 + (v_fine[...] % OVER).astype(F32) / OVER
    distance = (offset.astype(F32) - shift) / 0.6
    wv = jnp.exp(-0.5 * distance * distance)
    wv = jnp.where((offset >= 0) & (offset < KS), wv, 0.0)

    wait(recv_sem, 2, r_c)

    cells = r_c[...].astype(F32).reshape(plan.xg, span, plan.q)
    cells = jnp.concatenate([cells[g] for g in range(plan.xg)], axis=1).T
    cells = cells.reshape(plan.xg, plan.cv, plan.res, span)
    cells = [cells[:, i].reshape(part, span) for i in range(plan.cv)]
    cells = jnp.concatenate(cells, axis=1)
    time = lax.broadcasted_iota(jnp.int32, cells.shape, 1) & 7
    cells = jnp.concatenate([jnp.where(time == t, cells, 0.0) for t in range(8)], axis=0)
    along = tn(cells.astype(BF16), wu[...]) * wv
    middle = shape[0] // 2
    live = lax.broadcasted_iota(jnp.int32, (1, shape[1]), 1) < count[...]
    real = jnp.where(live, observed[0] - jnp.sum(along[:middle], axis=0, keepdims=True), 0.0)
    imag = jnp.where(live, observed[1] - jnp.sum(along[middle:], axis=0, keepdims=True), 0.0)
    res[0] = real
    res[1] = imag
    kept = pltpu.make_async_copy(res, res_out, load_sem.at[0])
    kept.start()
    row = lax.broadcasted_iota(jnp.int32, shape, 0)
    spread = (wv * jnp.where(row < middle, real, imag)).astype(BF16)
    both = nt(wu[...], spread)
    regrid = both[:part]
    for t in range(1, 8):
        regrid = jnp.where(time == t, both[t * part : (t + 1) * part], regrid)
    regrid = [regrid[:, i * span : (i + 1) * span] for i in range(plan.cv)]
    regrid = [one.reshape(plan.xg, 1, plan.res, span) for one in regrid]
    regrid = jnp.concatenate(regrid, axis=1).reshape(plan.xg * plan.q, span).T
    regrid = [regrid[:, g * plan.q : (g + 1) * plan.q] for g in range(plan.xg)]
    regrid = jnp.concatenate(regrid, axis=0)
    s_d[...] = regrid.reshape(devices, 8, plan.q).astype(BF16)
    send(3, s_d, r_d)
    wait(recv_sem, 3, r_d)

    cells = r_d[...].astype(F32).reshape(half, plan.q).astype(BF16)
    a = tn(cells, tch[...]) - swapped(tn(cells, tsh[...]))
    a = a * tw_c - swapped(a) * tw_s
    for g in range(plan.xg):
        s_e[g] = a[:, g * 128 : (g + 1) * 128].astype(BF16)
    across(4, s_e, r_e)
    wait(recv_sem, 4, r_e)

    data = r_e[...].reshape(plan.xg * plan.q, 128)
    total = jnp.dot(back[...], data, preferred_element_type=F32)
    s_f[...] = total.reshape(devices, 8, 128).astype(BF16)
    send(5, s_f, r_f, local=True)
    own = pltpu.make_async_copy(s_f.at[me], r_f.at[me], load_sem.at[1])
    own.start()
    wait(recv_sem, 5, r_f)
    own.wait()
    kept.wait()

    for phase, sent in enumerate((r_a, r_b, r_c, r_d, r_e, r_f, r_p)):
        wait(send_sem, phase, sent)


def finish(plan, residual, got, res_out, image_out, image, slots):
    res_out[...] = residual[...]
    tiles = image_out.shape[2] // 128
    per = 128 // plan.xl
    lane = lax.broadcasted_iota(jnp.int32, (plan.vg, 128), 1)
    slots[...] = got[...].astype(F32).reshape(plan.devices * 8, 128)
    for c in range(2):
        for k in range(plan.rl):
            for v in range(plan.v2):
                for g in range(0, plan.xg, per):
                    value = slots[rows(plan, c, k, v, g), :]
                    for n in range(1, per):
                        more = pltpu.roll(slots[rows(plan, c, k, v, g + n), :], n * plan.xl, 1)
                        value = jnp.where(lane < n * plan.xl, value, more)
                    tile = (k * SG + g * plan.xl) // 128
                    image[c, tile, pl.ds(v, plan.vg, stride=plan.v2), :] = value
    for k in range(tiles):
        image_out[:, :, k * 128 : (k + 1) * 128] = image[:, k]


def shards(facet_data, subgrid_pos, vis_counts, vis_u_fine, vis_v_fine, vis_observed):
    nsub = lax.axis_size("sub")
    devices = lax.axis_size("facet") * nsub
    plan = Plan(devices, nsub, facet_data.shape[1], facet_data.shape[2])
    slots = vis_u_fine.shape[1]

    table = block_transform(plan)
    high = table.astype(BF16)
    low = (table - high.astype(np.float32)).astype(BF16)

    wide = pltpu.VMEM((plan.xg, plan.q, 128), F32)
    narrow = pltpu.VMEM((plan.xg, plan.q, 128), BF16)
    tile = pltpu.VMEM((devices, 8, 128), BF16)
    cell = pltpu.VMEM((devices, 8, plan.q), BF16)
    turn = pltpu.VMEM((devices * 8, plan.x), BF16)
    rows_v, columns = facet_data.shape[1:]
    operands = (
        facet_data, subgrid_pos.reshape(1, 1), vis_u_fine, vis_v_fine, vis_observed,
        vis_counts.reshape(1, 1), jnp.asarray(high), jnp.asarray(low), jnp.asarray(high.T),
    )
    residual, got = pl.pallas_call(
        functools.partial(kernel, plan),
        out_shape=(
            jax.ShapeDtypeStruct(vis_observed.shape, F32),
            jax.ShapeDtypeStruct((devices, 8, 128), BF16),
        ),
        in_specs=[pl.BlockSpec(memory_space=pltpu.HBM)] * 9,
        out_specs=(pl.BlockSpec(memory_space=pltpu.HBM),) * 2,
        scratch_shapes=[
            pltpu.VMEM((2, columns // 128, rows_v, 128), F32),
            pltpu.VMEM((devices * 8, 128), F32),
            tile, tile,
            pltpu.VMEM((1, 128), jnp.int32),
            pltpu.VMEM((devices, 1, 128), jnp.int32),
            wide, wide, cell, cell, cell, cell, narrow, narrow, tile,
            pltpu.VMEM(vis_observed.shape, F32),
            pltpu.VMEM((8 * plan.nb, slots), BF16),
            turn, turn, turn, turn,
            pltpu.SemaphoreType.DMA((7,)),
            pltpu.SemaphoreType.DMA((7,)),
            pltpu.SemaphoreType.DMA((9,)),
        ]
        + [pltpu.VMEM(one.shape, one.dtype) for one in operands],
        compiler_params=pltpu.CompilerParams(
            collective_id=0, has_side_effects=True, vmem_limit_bytes=64 * 1024 * 1024 - 65536
        ),
    )(*operands)
    return pl.pallas_call(
        functools.partial(finish, plan),
        out_shape=(
            jax.ShapeDtypeStruct(vis_observed.shape, F32),
            jax.ShapeDtypeStruct(facet_data.shape, F32),
        ),
        in_specs=[pl.BlockSpec(memory_space=pltpu.VMEM)] * 2,
        out_specs=(pl.BlockSpec(memory_space=pltpu.VMEM),) * 2,
        scratch_shapes=[
            pltpu.VMEM((2, columns // 128, rows_v, 128), F32),
            pltpu.VMEM((devices * 8, 128), F32),
        ],
        compiler_params=pltpu.CompilerParams(vmem_limit_bytes=64 * 1024 * 1024 - 65536),
    )(residual, got)


def solution(mesh):
    return jax.shard_map(
        shards,
        mesh=mesh,
        in_specs=(
            P(None, None, ("facet", "sub")),
            P(("facet", "sub")),
            P(("facet", "sub")),
            P(("facet", "sub"), None),
            P(("facet", "sub"), None),
            P(None, ("facet", "sub"), None),
        ),
        out_specs=(P(None, ("facet", "sub"), None), P(None, None, ("facet", "sub"))),
        check_vma=False,
    )
```

```python
import functools
import math

import jax
import jax.numpy as jnp
import numpy as np
from jax import lax
from jax.experimental import pallas as pl
from jax.experimental.pallas import tpu as pltpu
from jax.sharding import PartitionSpec as P

SG = 512
KS = 8
OVER = 16
MESH = pl.DeviceIdType.MESH
F32 = jnp.float32
BF16 = jnp.bfloat16
COSINE = [(-1) ** k / math.factorial(2 * k) for k in range(9)]
SINE = [(-1) ** k / math.factorial(2 * k + 1) for k in range(8)]


class Plan:
    def __init__(self, devices, nsub, rows_v, columns):
        self.devices = devices
        self.nsub = nsub
        self.rows_v = rows_v
        self.width = columns * devices
        self.nb = self.width // SG
        self.rl = self.nb // devices
        self.vg = nsub
        self.xg = devices // nsub
        self.v2 = rows_v // self.vg
        self.xl = SG // self.xg
        self.res = self.nb // self.xg
        self.cv = 2 * self.v2
        self.q = self.cv * self.res
        self.x = self.xg * 128
        self.th = max(1, SG // self.nb // 4)
        self.rows = self.th * devices * 4
        self.partners = sorted(range(1, devices), key=lambda i: -(i % nsub))


def block_transform(plan):
    ids = np.arange(plan.nb)
    angle = 2.0 * np.pi * ((ids[:, None] * ids[None, :]) % plan.nb) / plan.nb
    cosine = np.cos(angle).reshape(plan.xg, plan.res, plan.devices, plan.rl)
    sine = np.sin(angle).reshape(plan.xg, plan.res, plan.devices, plan.rl)
    table = np.zeros((plan.xg, 2, plan.v2, plan.res, plan.devices, 2, 4), np.float32)
    for k in range(plan.rl):
        for v in range(plan.v2):
            into = k * plan.v2 + v
            table[:, 0, v, :, :, 0, into] = cosine[..., k]
            table[:, 0, v, :, :, 1, into] = sine[..., k]
            table[:, 1, v, :, :, 0, into] = -sine[..., k]
            table[:, 1, v, :, :, 1, into] = cosine[..., k]
    return table.reshape(plan.xg * plan.q, plan.devices * 8)


def nt(a, b):
    return lax.dot_general(a, b, (((1,), (1,)), ((), ())), preferred_element_type=F32)


def tn(a, b):
    return lax.dot_general(a, b, (((0,), (0,)), ((), ())), preferred_element_type=F32)


def split(a):
    high = a.astype(BF16)
    return high, (a - high.astype(F32)).astype(BF16)


def swapped(a):
    middle = a.shape[0] // 2
    return jnp.concatenate([a[middle:], -a[:middle]], axis=0)


def circle(p, period):
    h = p.astype(F32) * (2.0 * math.pi / period) - math.pi
    square = h * h
    cosine = jnp.full(h.shape, COSINE[-1], F32)
    for k in reversed(COSINE[:-1]):
        cosine = cosine * square + k
    sine = jnp.full(h.shape, SINE[-1], F32)
    for k in reversed(SINE[:-1]):
        sine = sine * square + k
    return -cosine, -sine * h


def to_rows(plan, a):
    step = a.shape[0] // plan.th
    return jnp.concatenate([a[h * step : (h + 1) * step] for h in range(plan.th)], axis=1)


def to_slots(plan, a):
    return to_rows(plan, a).reshape(plan.devices, 4, plan.th * plan.q)


def from_slots(plan, a, groups):
    a = a.astype(F32).reshape(plan.devices * 4, plan.th * plan.q)
    step = a.shape[0] // groups
    out = []
    for g in range(groups):
        for h in range(plan.th):
            out.append(a[g * step : (g + 1) * step, h * plan.q : (h + 1) * plan.q])
    return jnp.concatenate(out, axis=0)


def rows(plan, c, k, v, g):
    return pl.ds(g * plan.vg * 8 + c * 4 + k * plan.v2 + v, plan.vg, stride=8)


def kernel(plan, *refs):
    operands, (res_out, r_f) = refs[:9], refs[9:11]
    (
        image, slots, s_a, r_a, s_p, r_p, s_b, r_b, s_c, r_c, s_d, r_d, s_e, r_e, s_f,
        res, wu, tch, tcl, tsh, tsl, send_sem, recv_sem, load_sem,
    ) = refs[11:35]
    held = refs[35:]
    facet, position, u_fine, v_fine, observed, count, high, low, back = held
    devices, nsub = plan.devices, plan.nsub
    group, column = lax.axis_index("facet"), lax.axis_index("sub")
    me = group * nsub + column
    half = devices * 8

    loads = [
        pltpu.make_async_copy(operand, own, load_sem.at[n])
        for n, (operand, own) in enumerate(zip(operands, held))
    ]
    for load in loads:
        load.start()

    def place(i):
        target = me ^ i
        return target, (target // nsub, lax.rem(target, nsub))

    barrier = pltpu.get_barrier_semaphore()
    for i in plan.partners:
        pl.semaphore_signal(barrier, inc=1, device_id=place(i)[1], device_id_type=MESH)

    def send(phase, source, target, same=False, local=False):
        for i in plan.partners:
            to, device = place(i)
            pltpu.make_async_remote_copy(
                src_ref=source if same else source.at[to],
                dst_ref=target.at[me],
                send_sem=send_sem.at[phase],
                recv_sem=recv_sem.at[phase],
                device_id=device,
                device_id_type=MESH,
            ).start()
        if not local:
            target[me] = source[...] if same else source[me]

    def across(phase, source, target):
        for i in range(1, plan.xg):
            pltpu.make_async_remote_copy(
                src_ref=source.at[group ^ i],
                dst_ref=target.at[group],
                send_sem=send_sem.at[phase],
                recv_sem=recv_sem.at[phase],
                device_id=(group ^ i, column),
                device_id_type=MESH,
            ).start()
        target[group] = source[group]

    def wait(sem, phase, target):
        others = target.at[pl.ds(0, target.shape[0] - 1)]
        pltpu.make_async_copy(others, others, sem.at[phase]).wait()

    loads[0].wait()
    loads[1].wait()
    tiles = facet.shape[2] // 128
    per = 128 // plan.xl
    for k in range(tiles):
        image[:, k] = facet[:, :, k * 128 : (k + 1) * 128].astype(F32)
    slots[...] = jnp.zeros_like(slots)
    lane = lax.broadcasted_iota(jnp.int32, (plan.vg, 128), 1)

    for c in range(2):
        for k in range(plan.rl):
            for v in range(plan.v2):
                for g in range(plan.xg):
                    tile = (k * SG + g * plan.xl) // 128
                    value = image[c, tile, pl.ds(v, plan.vg, stride=plan.v2), :]
                    if per > 1:
                        if g % per:
                            value = pltpu.roll(value, 128 - (g % per) * plan.xl, 1)
                        value = jnp.where(lane < plan.xl, value, 0.0)
                    slots[rows(plan, c, k, v, g), :] = value
    s_a[...] = slots[...].reshape(devices, 8, 128).astype(BF16)
    s_p[...] = jnp.broadcast_to(position[...] // plan.nb, s_p.shape)

    pl.semaphore_wait(barrier, devices - 1)
    send(0, s_a, r_a)
    send(6, s_p, r_p, same=True)

    row = lax.broadcasted_iota(jnp.int32, (plan.res, plan.x), 0)
    lane8 = lax.broadcasted_iota(jnp.int32, (plan.res, plan.x), 1)
    x = (lane8 >> 7) * plan.xl + (lane8 & 127)
    tw_c, tw_s = circle((x * (group * plan.res + row)) & (plan.width - 1), plan.width)
    scale = 1.0 / math.sqrt(plan.width)
    tw_c = jnp.concatenate([tw_c * scale] * plan.cv, axis=0)
    tw_s = jnp.concatenate([tw_s * scale] * plan.cv, axis=0)

    for load in loads[2:]:
        load.wait()
    wait(recv_sem, 0, r_a)

    data = r_a[...].astype(F32).reshape(half, 128).astype(BF16)
    total = jnp.dot(high[...], data, preferred_element_type=F32)
    total += jnp.dot(low[...], data, preferred_element_type=F32)
    s_b[...] = total.reshape(plan.xg, plan.q, 128)
    across(1, s_b, r_b)

    wait(recv_sem, 6, r_p)
    base = jnp.broadcast_to(r_p[...], (devices, 4, 128)).reshape(devices * 4, 128)
    base = base + (lax.broadcasted_iota(jnp.int32, base.shape, 0) & 3)
    in_tile = lax.broadcasted_iota(jnp.int32, base.shape, 1)
    for h in range(plan.th):
        m = base + 4 * h
        at = pl.ds(h * devices * 4, devices * 4)
        for g in range(plan.xg):
            lanes = pl.ds(g * 128, 128)
            tc, ts = circle((m * (in_tile + g * plan.xl)) & (SG - 1), SG)
            tch[at, lanes], tcl[at, lanes] = split(tc)
            tsh[at, lanes], tsl[at, lanes] = split(ts)

    wait(recv_sem, 1, r_b)

    a = jnp.concatenate([r_b[g] for g in range(plan.xg)], axis=1)
    a = a * tw_c + swapped(a) * tw_s
    a_h, a_l = split(a)
    w_h, w_l = split(swapped(a))
    grid = nt(tch[...], a_h) + nt(tsh[...], w_h)
    grid += nt(tch[...], a_l) + nt(tsh[...], w_l)
    grid += nt(tcl[...], a_h) + nt(tsl[...], w_h)
    s_c[...] = to_slots(plan, grid).astype(BF16)
    send(2, s_c, r_c)

    cu = u_fine[...] // OVER
    shift = (KS - 1) / 2.0 + (u_fine[...] % OVER).astype(F32) / OVER
    part = plan.xg * plan.res
    for t in range(4 * plan.th):
        row = lax.broadcasted_iota(jnp.int32, (part, u_fine.shape[1]), 0)
        offset = row + plan.nb * t - cu
        distance = (offset.astype(F32) - shift) / 0.6
        weight = jnp.exp(-0.5 * distance * distance)
        weight = jnp.where((offset >= 0) & (offset < KS), weight, 0.0)
        wu[pl.ds(t * part, part), :] = weight.astype(BF16)

    span = plan.th * plan.vg * 4
    shape = (plan.cv * span, v_fine.shape[1])
    row = lax.broadcasted_iota(jnp.int32, shape, 0)
    v = lax.rem(lax.div(row, span), plan.v2) + lax.rem(row >> 2, plan.vg) * plan.v2
    offset = v - v_fine[...] // OVER
    shift = (KS - 1) / 2.0 + (v_fine[...] % OVER).astype(F32) / OVER
    distance = (offset.astype(F32) - shift) / 0.6
    wv = jnp.exp(-0.5 * distance * distance)
    wv = jnp.where((offset >= 0) & (offset < KS), wv, 0.0)

    wait(recv_sem, 2, r_c)

    cells = from_slots(plan, r_c[...], plan.xg)
    cells = cells.reshape(plan.xg, span, plan.q)
    cells = jnp.concatenate([cells[g] for g in range(plan.xg)], axis=1).T
    cells = cells.reshape(plan.xg, plan.cv, plan.res, span)
    cells = [cells[:, i].reshape(part, span) for i in range(plan.cv)]
    cells = jnp.concatenate(cells, axis=1)
    place_in = lax.rem(lax.broadcasted_iota(jnp.int32, cells.shape, 1), span)
    time = lax.div(place_in, plan.vg * 4) * 4 + (place_in & 3)
    times = range(4 * plan.th)
    cells = jnp.concatenate([jnp.where(time == t, cells, 0.0) for t in times], axis=0)
    along = tn(cells.astype(BF16), wu[...]) * wv
    middle = shape[0] // 2
    live = lax.broadcasted_iota(jnp.int32, (1, shape[1]), 1) < count[...]
    real = jnp.where(live, observed[0] - jnp.sum(along[:middle], axis=0, keepdims=True), 0.0)
    imag = jnp.where(live, observed[1] - jnp.sum(along[middle:], axis=0, keepdims=True), 0.0)
    res[0] = real
    res[1] = imag
    kept = pltpu.make_async_copy(res, res_out, load_sem.at[0])
    kept.start()
    row = lax.broadcasted_iota(jnp.int32, shape, 0)
    spread = (wv * jnp.where(row < middle, real, imag)).astype(BF16)
    both = nt(wu[...], spread)
    regrid = both[:part]
    for t in times[1:]:
        regrid = jnp.where(time == t, both[t * part : (t + 1) * part], regrid)
    regrid = [regrid[:, i * span : (i + 1) * span] for i in range(plan.cv)]
    regrid = [one.reshape(plan.xg, 1, plan.res, span) for one in regrid]
    regrid = jnp.concatenate(regrid, axis=1).reshape(plan.xg * plan.q, span).T
    regrid = [
        to_rows(plan, regrid[:, g * plan.q : (g + 1) * plan.q]) for g in range(plan.xg)
    ]
    regrid = jnp.concatenate(regrid, axis=0)
    s_d[...] = regrid.reshape(devices, 4, plan.th * plan.q).astype(BF16)
    send(3, s_d, r_d)
    wait(recv_sem, 3, r_d)

    cells = from_slots(plan, r_d[...], 1).astype(BF16)
    a = tn(cells, tch[...]) - swapped(tn(cells, tsh[...]))
    a = a * tw_c - swapped(a) * tw_s
    for g in range(plan.xg):
        s_e[g] = a[:, g * 128 : (g + 1) * 128].astype(BF16)
    across(4, s_e, r_e)
    wait(recv_sem, 4, r_e)

    data = r_e[...].reshape(plan.xg * plan.q, 128)
    total = jnp.dot(back[...], data, preferred_element_type=F32)
    s_f[...] = total.reshape(devices, 8, 128).astype(BF16)
    send(5, s_f, r_f, local=True)
    own = pltpu.make_async_copy(s_f.at[me], r_f.at[me], load_sem.at[1])
    own.start()
    wait(recv_sem, 5, r_f)
    own.wait()
    kept.wait()

    for phase, sent in enumerate((r_a, r_b, r_c, r_d, r_e, r_f, r_p)):
        wait(send_sem, phase, sent)


def finish(plan, residual, got, res_out, image_out, image, slots):
    res_out[...] = residual[...]
    tiles = image_out.shape[2] // 128
    per = 128 // plan.xl
    lane = lax.broadcasted_iota(jnp.int32, (plan.vg, 128), 1)
    slots[...] = got[...].astype(F32).reshape(plan.devices * 8, 128)
    for c in range(2):
        for k in range(plan.rl):
            for v in range(plan.v2):
                for g in range(0, plan.xg, per):
                    value = slots[rows(plan, c, k, v, g), :]
                    for n in range(1, per):
                        more = pltpu.roll(slots[rows(plan, c, k, v, g + n), :], n * plan.xl, 1)
                        value = jnp.where(lane < n * plan.xl, value, more)
                    tile = (k * SG + g * plan.xl) // 128
                    image[c, tile, pl.ds(v, plan.vg, stride=plan.v2), :] = value
    for k in range(tiles):
        image_out[:, :, k * 128 : (k + 1) * 128] = image[:, k]


def shards(facet_data, subgrid_pos, vis_counts, vis_u_fine, vis_v_fine, vis_observed):
    nsub = lax.axis_size("sub")
    devices = lax.axis_size("facet") * nsub
    plan = Plan(devices, nsub, facet_data.shape[1], facet_data.shape[2])
    slots = vis_u_fine.shape[1]

    table = block_transform(plan)
    high = table.astype(BF16)
    low = (table - high.astype(np.float32)).astype(BF16)

    wide = pltpu.VMEM((plan.xg, plan.q, 128), F32)
    narrow = pltpu.VMEM((plan.xg, plan.q, 128), BF16)
    tile = pltpu.VMEM((devices, 8, 128), BF16)
    cell = pltpu.VMEM((devices, 4, plan.th * plan.q), BF16)
    turn = pltpu.VMEM((plan.rows, plan.x), BF16)
    rows_v, columns = facet_data.shape[1:]
    operands = (
        facet_data, subgrid_pos.reshape(1, 1), vis_u_fine, vis_v_fine, vis_observed,
        vis_counts.reshape(1, 1), jnp.asarray(high), jnp.asarray(low), jnp.asarray(high.T),
    )
    residual, got = pl.pallas_call(
        functools.partial(kernel, plan),
        out_shape=(
            jax.ShapeDtypeStruct(vis_observed.shape, F32),
            jax.ShapeDtypeStruct((devices, 8, 128), BF16),
        ),
        in_specs=[pl.BlockSpec(memory_space=pltpu.HBM)] * 9,
        out_specs=(pl.BlockSpec(memory_space=pltpu.HBM),) * 2,
        scratch_shapes=[
            pltpu.VMEM((2, columns // 128, rows_v, 128), F32),
            pltpu.VMEM((devices * 8, 128), F32),
            tile, tile,
            pltpu.VMEM((1, 128), jnp.int32),
            pltpu.VMEM((devices, 1, 128), jnp.int32),
            wide, wide, cell, cell, cell, cell, narrow, narrow, tile,
            pltpu.VMEM(vis_observed.shape, F32),
            pltpu.VMEM((4 * plan.th * plan.nb, slots), BF16),
            turn, turn, turn, turn,
            pltpu.SemaphoreType.DMA((7,)),
            pltpu.SemaphoreType.DMA((7,)),
            pltpu.SemaphoreType.DMA((9,)),
        ]
        + [pltpu.VMEM(one.shape, one.dtype) for one in operands],
        compiler_params=pltpu.CompilerParams(
            collective_id=0, has_side_effects=True, vmem_limit_bytes=64 * 1024 * 1024 - 65536
        ),
    )(*operands)
    return pl.pallas_call(
        functools.partial(finish, plan),
        out_shape=(
            jax.ShapeDtypeStruct(vis_observed.shape, F32),
            jax.ShapeDtypeStruct(facet_data.shape, F32),
        ),
        in_specs=[pl.BlockSpec(memory_space=pltpu.VMEM)] * 2,
        out_specs=(pl.BlockSpec(memory_space=pltpu.VMEM),) * 2,
        scratch_shapes=[
            pltpu.VMEM((2, columns // 128, rows_v, 128), F32),
            pltpu.VMEM((devices * 8, 128), F32),
        ],
        compiler_params=pltpu.CompilerParams(vmem_limit_bytes=64 * 1024 * 1024 - 65536),
    )(residual, got)


def solution(mesh):
    return jax.shard_map(
        shards,
        mesh=mesh,
        in_specs=(
            P(None, None, ("facet", "sub")),
            P(("facet", "sub")),
            P(("facet", "sub")),
            P(("facet", "sub"), None),
            P(("facet", "sub"), None),
            P(None, ("facet", "sub"), None),
        ),
        out_specs=(P(None, ("facet", "sub"), None), P(None, None, ("facet", "sub"))),
        check_vma=False,
    )
```

```python
import functools
import math

import jax
import jax.numpy as jnp
import numpy as np
from jax import lax
from jax.experimental import pallas as pl
from jax.experimental.pallas import tpu as pltpu
from jax.sharding import PartitionSpec as P

SG = 512
KS = 8
OVER = 16
MESH = pl.DeviceIdType.MESH
F32 = jnp.float32
BF16 = jnp.bfloat16
COSINE = [(-1) ** k / math.factorial(2 * k) for k in range(9)]
SINE = [(-1) ** k / math.factorial(2 * k + 1) for k in range(8)]


class Plan:
    def __init__(self, devices, nsub, rows_v, columns):
        self.devices = devices
        self.nsub = nsub
        self.rows_v = rows_v
        self.width = columns * devices
        self.nb = self.width // SG
        self.rl = self.nb // devices
        self.vg = nsub
        self.xg = devices // nsub
        self.v2 = rows_v // self.vg
        self.xl = SG // self.xg
        self.res = self.nb // self.xg
        self.cv = 2 * self.v2
        self.q = self.cv * self.res
        self.x = self.xg * 128
        self.th = max(1, SG // self.nb // 4)
        self.rows = self.th * devices * 4
        self.partners = sorted(range(1, devices), key=lambda i: -(i % nsub))


def block_transform(plan):
    ids = np.arange(plan.nb)
    angle = 2.0 * np.pi * ((ids[:, None] * ids[None, :]) % plan.nb) / plan.nb
    cosine = np.cos(angle).reshape(plan.xg, plan.res, plan.devices, plan.rl)
    sine = np.sin(angle).reshape(plan.xg, plan.res, plan.devices, plan.rl)
    table = np.zeros((plan.xg, 2, plan.v2, plan.res, plan.devices, 2, 4), np.float32)
    for k in range(plan.rl):
        for v in range(plan.v2):
            into = k * plan.v2 + v
            table[:, 0, v, :, :, 0, into] = cosine[..., k]
            table[:, 0, v, :, :, 1, into] = sine[..., k]
            table[:, 1, v, :, :, 0, into] = -sine[..., k]
            table[:, 1, v, :, :, 1, into] = cosine[..., k]
    return table.reshape(plan.xg * plan.q, plan.devices * 8)


def nt(a, b):
    return lax.dot_general(a, b, (((1,), (1,)), ((), ())), preferred_element_type=F32)


def tn(a, b):
    return lax.dot_general(a, b, (((0,), (0,)), ((), ())), preferred_element_type=F32)


def split(a):
    high = a.astype(BF16)
    return high, (a - high.astype(F32)).astype(BF16)


def swapped(a):
    middle = a.shape[0] // 2
    return jnp.concatenate([a[middle:], -a[:middle]], axis=0)


def circle(p, period):
    h = p.astype(F32) * (2.0 * math.pi / period) - math.pi
    square = h * h
    cosine = jnp.full(h.shape, COSINE[-1], F32)
    for k in reversed(COSINE[:-1]):
        cosine = cosine * square + k
    sine = jnp.full(h.shape, SINE[-1], F32)
    for k in reversed(SINE[:-1]):
        sine = sine * square + k
    return -cosine, -sine * h


def to_rows(plan, a):
    step = a.shape[0] // plan.th
    return jnp.concatenate([a[h * step : (h + 1) * step] for h in range(plan.th)], axis=1)


def to_slots(plan, a):
    return to_rows(plan, a).reshape(plan.devices, 4, plan.th * plan.q)


def from_slots(plan, a, groups):
    a = a.astype(F32).reshape(plan.devices * 4, plan.th * plan.q)
    step = a.shape[0] // groups
    out = []
    for g in range(groups):
        for h in range(plan.th):
            out.append(a[g * step : (g + 1) * step, h * plan.q : (h + 1) * plan.q])
    return jnp.concatenate(out, axis=0)


def rows(plan, c, k, v, g):
    return pl.ds(g * plan.vg * 8 + c * 4 + k * plan.v2 + v, plan.vg, stride=8)


def kernel(plan, *refs):
    operands, (res_out, r_f) = refs[:9], refs[9:11]
    (
        image, slots, s_a, r_a, s_p, g_p, r_p, s_b, r_b, s_c, r_c, s_d, r_d, s_e, r_e, s_f,
        res, wu, tch, tcl, tsh, tsl, send_sem, recv_sem, load_sem,
    ) = refs[11:36]
    held = refs[36:]
    facet, position, u_fine, v_fine, observed, count, high, low, back = held
    devices, nsub = plan.devices, plan.nsub
    group, column = lax.axis_index("facet"), lax.axis_index("sub")
    me = group * nsub + column
    half = devices * 8

    loads = [
        pltpu.make_async_copy(operand, own, load_sem.at[n])
        for n, (operand, own) in enumerate(zip(operands, held))
    ]
    for load in loads:
        load.start()

    def place(i):
        target = me ^ i
        return target, (target // nsub, lax.rem(target, nsub))

    barrier = pltpu.get_barrier_semaphore()
    for i in plan.partners:
        pl.semaphore_signal(barrier, inc=1, device_id=place(i)[1], device_id_type=MESH)

    def send(phase, source, target, local=False):
        for i in plan.partners:
            to, device = place(i)
            pltpu.make_async_remote_copy(
                src_ref=source.at[to],
                dst_ref=target.at[me],
                send_sem=send_sem.at[phase],
                recv_sem=recv_sem.at[phase],
                device_id=device,
                device_id_type=MESH,
            ).start()
        if not local:
            target[me] = source[me]

    def share(phase, source, target, own, partners):
        for device in partners:
            pltpu.make_async_remote_copy(
                src_ref=source,
                dst_ref=target.at[own],
                send_sem=send_sem.at[phase],
                recv_sem=recv_sem.at[phase],
                device_id=device,
                device_id_type=MESH,
            ).start()
        target[own] = source[...]

    def across(phase, source, target):
        for i in range(1, plan.xg):
            pltpu.make_async_remote_copy(
                src_ref=source.at[group ^ i],
                dst_ref=target.at[group],
                send_sem=send_sem.at[phase],
                recv_sem=recv_sem.at[phase],
                device_id=(group ^ i, column),
                device_id_type=MESH,
            ).start()
        target[group] = source[group]

    def wait(sem, phase, target):
        others = target.at[pl.ds(0, target.shape[0] - 1)]
        pltpu.make_async_copy(others, others, sem.at[phase]).wait()

    loads[0].wait()
    loads[1].wait()
    tiles = facet.shape[2] // 128
    per = 128 // plan.xl
    for k in range(tiles):
        image[:, k] = facet[:, :, k * 128 : (k + 1) * 128].astype(F32)
    slots[...] = jnp.zeros_like(slots)
    lane = lax.broadcasted_iota(jnp.int32, (plan.vg, 128), 1)

    for c in range(2):
        for k in range(plan.rl):
            for v in range(plan.v2):
                for g in range(plan.xg):
                    tile = (k * SG + g * plan.xl) // 128
                    value = image[c, tile, pl.ds(v, plan.vg, stride=plan.v2), :]
                    if per > 1:
                        if g % per:
                            value = pltpu.roll(value, 128 - (g % per) * plan.xl, 1)
                        value = jnp.where(lane < plan.xl, value, 0.0)
                    slots[rows(plan, c, k, v, g), :] = value
    s_a[...] = slots[...].reshape(devices, 8, 128).astype(BF16)
    s_p[...] = jnp.broadcast_to(position[...] // plan.nb, s_p.shape)

    pl.semaphore_wait(barrier, devices - 1)
    share(6, s_p, g_p, group, [(group ^ i, column) for i in range(1, plan.xg)])
    send(0, s_a, r_a)
    wait(recv_sem, 6, g_p)
    share(7, g_p, r_p, column, [(group, column ^ i) for i in range(1, nsub)])

    row = lax.broadcasted_iota(jnp.int32, (plan.res, plan.x), 0)
    lane8 = lax.broadcasted_iota(jnp.int32, (plan.res, plan.x), 1)
    x = (lane8 >> 7) * plan.xl + (lane8 & 127)
    tw_c, tw_s = circle((x * (group * plan.res + row)) & (plan.width - 1), plan.width)
    scale = 1.0 / math.sqrt(plan.width)
    tw_c = jnp.concatenate([tw_c * scale] * plan.cv, axis=0)
    tw_s = jnp.concatenate([tw_s * scale] * plan.cv, axis=0)

    for load in loads[2:]:
        load.wait()
    wait(recv_sem, 0, r_a)

    data = r_a[...].astype(F32).reshape(half, 128).astype(BF16)
    total = jnp.dot(high[...], data, preferred_element_type=F32)
    total += jnp.dot(low[...], data, preferred_element_type=F32)
    s_b[...] = total.reshape(plan.xg, plan.q, 128)
    across(1, s_b, r_b)

    wait(recv_sem, 7, r_p)
    base = jnp.concatenate([r_p[:, g] for g in range(plan.xg)], axis=0)
    base = jnp.broadcast_to(base, (devices, 4, 128)).reshape(devices * 4, 128)
    base = base + (lax.broadcasted_iota(jnp.int32, base.shape, 0) & 3)
    in_tile = lax.broadcasted_iota(jnp.int32, base.shape, 1)
    for h in range(plan.th):
        m = base + 4 * h
        at = pl.ds(h * devices * 4, devices * 4)
        for g in range(plan.xg):
            lanes = pl.ds(g * 128, 128)
            tc, ts = circle((m * (in_tile + g * plan.xl)) & (SG - 1), SG)
            tch[at, lanes], tcl[at, lanes] = split(tc)
            tsh[at, lanes], tsl[at, lanes] = split(ts)

    wait(recv_sem, 1, r_b)

    a = jnp.concatenate([r_b[g] for g in range(plan.xg)], axis=1)
    a = a * tw_c + swapped(a) * tw_s
    a_h, a_l = split(a)
    w_h, w_l = split(swapped(a))
    grid = nt(tch[...], a_h) + nt(tsh[...], w_h)
    grid += nt(tch[...], a_l) + nt(tsh[...], w_l)
    grid += nt(tcl[...], a_h) + nt(tsl[...], w_h)
    s_c[...] = to_slots(plan, grid).astype(BF16)
    send(2, s_c, r_c)

    cu = u_fine[...] // OVER
    shift = (KS - 1) / 2.0 + (u_fine[...] % OVER).astype(F32) / OVER
    part = plan.xg * plan.res
    for t in range(4 * plan.th):
        row = lax.broadcasted_iota(jnp.int32, (part, u_fine.shape[1]), 0)
        offset = row + plan.nb * t - cu
        distance = (offset.astype(F32) - shift) / 0.6
        weight = jnp.exp(-0.5 * distance * distance)
        weight = jnp.where((offset >= 0) & (offset < KS), weight, 0.0)
        wu[pl.ds(t * part, part), :] = weight.astype(BF16)

    span = plan.th * plan.vg * 4
    shape = (plan.cv * span, v_fine.shape[1])
    row = lax.broadcasted_iota(jnp.int32, shape, 0)
    v = lax.rem(lax.div(row, span), plan.v2) + lax.rem(row >> 2, plan.vg) * plan.v2
    offset = v - v_fine[...] // OVER
    shift = (KS - 1) / 2.0 + (v_fine[...] % OVER).astype(F32) / OVER
    distance = (offset.astype(F32) - shift) / 0.6
    wv = jnp.exp(-0.5 * distance * distance)
    wv = jnp.where((offset >= 0) & (offset < KS), wv, 0.0)

    wait(recv_sem, 2, r_c)

    cells = from_slots(plan, r_c[...], plan.xg)
    cells = cells.reshape(plan.xg, span, plan.q)
    cells = jnp.concatenate([cells[g] for g in range(plan.xg)], axis=1).T
    cells = cells.reshape(plan.xg, plan.cv, plan.res, span)
    cells = [cells[:, i].reshape(part, span) for i in range(plan.cv)]
    cells = jnp.concatenate(cells, axis=1)
    place_in = lax.rem(lax.broadcasted_iota(jnp.int32, cells.shape, 1), span)
    time = lax.div(place_in, plan.vg * 4) * 4 + (place_in & 3)
    times = range(4 * plan.th)
    cells = jnp.concatenate([jnp.where(time == t, cells, 0.0) for t in times], axis=0)
    along = tn(cells.astype(BF16), wu[...]) * wv
    middle = shape[0] // 2
    live = lax.broadcasted_iota(jnp.int32, (1, shape[1]), 1) < count[...]
    real = jnp.where(live, observed[0] - jnp.sum(along[:middle], axis=0, keepdims=True), 0.0)
    imag = jnp.where(live, observed[1] - jnp.sum(along[middle:], axis=0, keepdims=True), 0.0)
    res[0] = real
    res[1] = imag
    kept = pltpu.make_async_copy(res, res_out, load_sem.at[0])
    kept.start()
    row = lax.broadcasted_iota(jnp.int32, shape, 0)
    spread = (wv * jnp.where(row < middle, real, imag)).astype(BF16)
    both = nt(wu[...], spread)
    regrid = both[:part]
    for t in times[1:]:
        regrid = jnp.where(time == t, both[t * part : (t + 1) * part], regrid)
    regrid = [regrid[:, i * span : (i + 1) * span] for i in range(plan.cv)]
    regrid = [one.reshape(plan.xg, 1, plan.res, span) for one in regrid]
    regrid = jnp.concatenate(regrid, axis=1).reshape(plan.xg * plan.q, span).T
    regrid = [
        to_rows(plan, regrid[:, g * plan.q : (g + 1) * plan.q]) for g in range(plan.xg)
    ]
    regrid = jnp.concatenate(regrid, axis=0)
    s_d[...] = regrid.reshape(devices, 4, plan.th * plan.q).astype(BF16)
    send(3, s_d, r_d)
    wait(recv_sem, 3, r_d)

    cells = from_slots(plan, r_d[...], 1).astype(BF16)
    a = tn(cells, tch[...]) - swapped(tn(cells, tsh[...]))
    a = a * tw_c - swapped(a) * tw_s
    for g in range(plan.xg):
        s_e[g] = a[:, g * 128 : (g + 1) * 128].astype(BF16)
    across(4, s_e, r_e)
    wait(recv_sem, 4, r_e)

    data = r_e[...].reshape(plan.xg * plan.q, 128)
    total = jnp.dot(back[...], data, preferred_element_type=F32)
    s_f[...] = total.reshape(devices, 8, 128).astype(BF16)
    send(5, s_f, r_f, local=True)
    own = pltpu.make_async_copy(s_f.at[me], r_f.at[me], load_sem.at[1])
    own.start()
    wait(recv_sem, 5, r_f)
    own.wait()
    kept.wait()

    for phase, sent in enumerate((r_a, r_b, r_c, r_d, r_e, r_f, g_p, r_p)):
        wait(send_sem, phase, sent)


def finish(plan, residual, got, res_out, image_out, image, slots):
    res_out[...] = residual[...]
    tiles = image_out.shape[2] // 128
    per = 128 // plan.xl
    lane = lax.broadcasted_iota(jnp.int32, (plan.vg, 128), 1)
    slots[...] = got[...].astype(F32).reshape(plan.devices * 8, 128)
    for c in range(2):
        for k in range(plan.rl):
            for v in range(plan.v2):
                for g in range(0, plan.xg, per):
                    value = slots[rows(plan, c, k, v, g), :]
                    for n in range(1, per):
                        more = pltpu.roll(slots[rows(plan, c, k, v, g + n), :], n * plan.xl, 1)
                        value = jnp.where(lane < n * plan.xl, value, more)
                    tile = (k * SG + g * plan.xl) // 128
                    image[c, tile, pl.ds(v, plan.vg, stride=plan.v2), :] = value
    for k in range(tiles):
        image_out[:, :, k * 128 : (k + 1) * 128] = image[:, k]


def shards(facet_data, subgrid_pos, vis_counts, vis_u_fine, vis_v_fine, vis_observed):
    nsub = lax.axis_size("sub")
    devices = lax.axis_size("facet") * nsub
    plan = Plan(devices, nsub, facet_data.shape[1], facet_data.shape[2])
    slots = vis_u_fine.shape[1]

    table = block_transform(plan)
    high = table.astype(BF16)
    low = (table - high.astype(np.float32)).astype(BF16)

    wide = pltpu.VMEM((plan.xg, plan.q, 128), F32)
    narrow = pltpu.VMEM((plan.xg, plan.q, 128), BF16)
    tile = pltpu.VMEM((devices, 8, 128), BF16)
    cell = pltpu.VMEM((devices, 4, plan.th * plan.q), BF16)
    turn = pltpu.VMEM((plan.rows, plan.x), BF16)
    rows_v, columns = facet_data.shape[1:]
    operands = (
        facet_data, subgrid_pos.reshape(1, 1), vis_u_fine, vis_v_fine, vis_observed,
        vis_counts.reshape(1, 1), jnp.asarray(high), jnp.asarray(low), jnp.asarray(high.T),
    )
    residual, got = pl.pallas_call(
        functools.partial(kernel, plan),
        out_shape=(
            jax.ShapeDtypeStruct(vis_observed.shape, F32),
            jax.ShapeDtypeStruct((devices, 8, 128), BF16),
        ),
        in_specs=[pl.BlockSpec(memory_space=pltpu.HBM)] * 9,
        out_specs=(pl.BlockSpec(memory_space=pltpu.HBM),) * 2,
        scratch_shapes=[
            pltpu.VMEM((2, columns // 128, rows_v, 128), F32),
            pltpu.VMEM((devices * 8, 128), F32),
            tile, tile,
            pltpu.VMEM((1, 128), jnp.int32),
            pltpu.VMEM((plan.xg, 1, 128), jnp.int32),
            pltpu.VMEM((nsub, plan.xg, 1, 128), jnp.int32),
            wide, wide, cell, cell, cell, cell, narrow, narrow, tile,
            pltpu.VMEM(vis_observed.shape, F32),
            pltpu.VMEM((4 * plan.th * plan.nb, slots), BF16),
            turn, turn, turn, turn,
            pltpu.SemaphoreType.DMA((8,)),
            pltpu.SemaphoreType.DMA((8,)),
            pltpu.SemaphoreType.DMA((9,)),
        ]
        + [pltpu.VMEM(one.shape, one.dtype) for one in operands],
        compiler_params=pltpu.CompilerParams(
            collective_id=0, has_side_effects=True, vmem_limit_bytes=64 * 1024 * 1024 - 65536
        ),
    )(*operands)
    return pl.pallas_call(
        functools.partial(finish, plan),
        out_shape=(
            jax.ShapeDtypeStruct(vis_observed.shape, F32),
            jax.ShapeDtypeStruct(facet_data.shape, F32),
        ),
        in_specs=[pl.BlockSpec(memory_space=pltpu.VMEM)] * 2,
        out_specs=(pl.BlockSpec(memory_space=pltpu.VMEM),) * 2,
        scratch_shapes=[
            pltpu.VMEM((2, columns // 128, rows_v, 128), F32),
            pltpu.VMEM((devices * 8, 128), F32),
        ],
        compiler_params=pltpu.CompilerParams(vmem_limit_bytes=64 * 1024 * 1024 - 65536),
    )(residual, got)


def solution(mesh):
    return jax.shard_map(
        shards,
        mesh=mesh,
        in_specs=(
            P(None, None, ("facet", "sub")),
            P(("facet", "sub")),
            P(("facet", "sub")),
            P(("facet", "sub"), None),
            P(("facet", "sub"), None),
            P(None, ("facet", "sub"), None),
        ),
        out_specs=(P(None, ("facet", "sub"), None), P(None, None, ("facet", "sub"))),
        check_vma=False,
    )
```

```python
import functools
import math

import jax
import jax.numpy as jnp
import numpy as np
from jax import lax
from jax.experimental import pallas as pl
from jax.experimental.pallas import tpu as pltpu
from jax.sharding import PartitionSpec as P

SG = 512
KS = 8
OVER = 16
MESH = pl.DeviceIdType.MESH
F32 = jnp.float32
BF16 = jnp.bfloat16
COSINE = [(-1) ** k / math.factorial(2 * k) for k in range(9)]
SINE = [(-1) ** k / math.factorial(2 * k + 1) for k in range(8)]


class Plan:
    def __init__(self, devices, nsub, rows_v, columns):
        self.devices = devices
        self.nsub = nsub
        self.rows_v = rows_v
        self.width = columns * devices
        self.nb = self.width // SG
        self.rl = self.nb // devices
        self.vg = nsub
        self.xg = devices // nsub
        self.v2 = rows_v // self.vg
        self.xl = SG // self.xg
        self.res = self.nb // self.xg
        self.cv = 2 * self.v2
        self.q = self.cv * self.res
        self.x = self.xg * 128
        self.th = max(1, SG // self.nb // 4)
        self.rows = self.th * devices * 4
        self.partners = sorted(range(1, devices), key=lambda i: -(i % nsub))


def block_transform(plan):
    ids = np.arange(plan.nb)
    angle = 2.0 * np.pi * ((ids[:, None] * ids[None, :]) % plan.nb) / plan.nb
    cosine = np.cos(angle).reshape(plan.xg, plan.res, plan.devices, plan.rl)
    sine = np.sin(angle).reshape(plan.xg, plan.res, plan.devices, plan.rl)
    table = np.zeros((plan.xg, 2, plan.v2, plan.res, plan.devices, 2, 4), np.float32)
    for k in range(plan.rl):
        for v in range(plan.v2):
            into = k * plan.v2 + v
            table[:, 0, v, :, :, 0, into] = cosine[..., k]
            table[:, 0, v, :, :, 1, into] = sine[..., k]
            table[:, 1, v, :, :, 0, into] = -sine[..., k]
            table[:, 1, v, :, :, 1, into] = cosine[..., k]
    return table.reshape(plan.xg * plan.q, plan.devices * 8)


def nt(a, b):
    return lax.dot_general(a, b, (((1,), (1,)), ((), ())), preferred_element_type=F32)


def tn(a, b):
    return lax.dot_general(a, b, (((0,), (0,)), ((), ())), preferred_element_type=F32)


def split(a):
    high = a.astype(BF16)
    return high, (a - high.astype(F32)).astype(BF16)


def swapped(a):
    middle = a.shape[0] // 2
    return jnp.concatenate([a[middle:], -a[:middle]], axis=0)


def circle(p, period):
    h = p.astype(F32) * (2.0 * math.pi / period) - math.pi
    square = h * h
    cosine = jnp.full(h.shape, COSINE[-1], F32)
    for k in reversed(COSINE[:-1]):
        cosine = cosine * square + k
    sine = jnp.full(h.shape, SINE[-1], F32)
    for k in reversed(SINE[:-1]):
        sine = sine * square + k
    return -cosine, -sine * h


def to_rows(plan, a):
    step = a.shape[0] // plan.th
    return jnp.concatenate([a[h * step : (h + 1) * step] for h in range(plan.th)], axis=1)


def to_slots(plan, a):
    return to_rows(plan, a).reshape(plan.devices, 4, plan.th * plan.q)


def from_slots(plan, a, groups):
    a = a.astype(F32).reshape(plan.devices * 4, plan.th * plan.q)
    step = a.shape[0] // groups
    out = []
    for g in range(groups):
        for h in range(plan.th):
            out.append(a[g * step : (g + 1) * step, h * plan.q : (h + 1) * plan.q])
    return jnp.concatenate(out, axis=0)


def rows(plan, c, k, v, g):
    return pl.ds(g * plan.vg * 8 + c * 4 + k * plan.v2 + v, plan.vg, stride=8)


def kernel(plan, *refs):
    operands, (res_out, r_f) = refs[:9], refs[9:11]
    (
        image, slots, s_a, r_a, s_p, r_p, s_b, r_b, s_c, r_c, s_d, r_d, s_e, r_e, s_f,
        res, wu, tch, tcl, tsh, tsl, send_sem, recv_sem, load_sem,
    ) = refs[11:35]
    held = refs[35:]
    facet, position, u_fine, v_fine, observed, count, high, low, back = held
    devices, nsub = plan.devices, plan.nsub
    group, column = lax.axis_index("facet"), lax.axis_index("sub")
    me = group * nsub + column
    half = devices * 8

    loads = [
        pltpu.make_async_copy(operand, own, load_sem.at[n])
        for n, (operand, own) in enumerate(zip(operands, held))
    ]
    for load in loads:
        load.start()

    def place(i):
        target = me ^ i
        return target, (target // nsub, lax.rem(target, nsub))

    barrier = pltpu.get_barrier_semaphore()
    for i in plan.partners:
        pl.semaphore_signal(barrier, inc=1, device_id=place(i)[1], device_id_type=MESH)

    def send(phase, source, target, same=False, local=False):
        for i in plan.partners:
            to, device = place(i)
            pltpu.make_async_remote_copy(
                src_ref=source if same else source.at[to],
                dst_ref=target.at[me],
                send_sem=send_sem.at[phase],
                recv_sem=recv_sem.at[phase],
                device_id=device,
                device_id_type=MESH,
            ).start()
        if not local:
            target[me] = source[...] if same else source[me]

    def across(phase, source, target):
        for i in range(1, plan.xg):
            pltpu.make_async_remote_copy(
                src_ref=source.at[group ^ i],
                dst_ref=target.at[group],
                send_sem=send_sem.at[phase],
                recv_sem=recv_sem.at[phase],
                device_id=(group ^ i, column),
                device_id_type=MESH,
            ).start()
        target[group] = source[group]

    def wait(sem, phase, target):
        others = target.at[pl.ds(0, target.shape[0] - 1)]
        pltpu.make_async_copy(others, others, sem.at[phase]).wait()

    loads[0].wait()
    loads[1].wait()
    tiles = facet.shape[2] // 128
    per = 128 // plan.xl
    for k in range(tiles):
        image[:, k] = facet[:, :, k * 128 : (k + 1) * 128].astype(F32)
    slots[...] = jnp.zeros_like(slots)
    lane = lax.broadcasted_iota(jnp.int32, (plan.vg, 128), 1)

    for c in range(2):
        for k in range(plan.rl):
            for v in range(plan.v2):
                for g in range(plan.xg):
                    tile = (k * SG + g * plan.xl) // 128
                    value = image[c, tile, pl.ds(v, plan.vg, stride=plan.v2), :]
                    if per > 1:
                        if g % per:
                            value = pltpu.roll(value, 128 - (g % per) * plan.xl, 1)
                        value = jnp.where(lane < plan.xl, value, 0.0)
                    slots[rows(plan, c, k, v, g), :] = value
    s_a[...] = slots[...].reshape(devices, 8, 128).astype(BF16)
    s_p[...] = jnp.broadcast_to(position[...] // plan.nb, s_p.shape)

    pl.semaphore_wait(barrier, devices - 1)
    send(0, s_a, r_a)
    send(6, s_p, r_p, same=True)

    row = lax.broadcasted_iota(jnp.int32, (plan.res, plan.x), 0)
    lane8 = lax.broadcasted_iota(jnp.int32, (plan.res, plan.x), 1)
    x = (lane8 >> 7) * plan.xl + (lane8 & 127)
    tw_c, tw_s = circle((x * (group * plan.res + row)) & (plan.width - 1), plan.width)
    scale = 1.0 / math.sqrt(plan.width)
    tw_c = jnp.concatenate([tw_c * scale] * plan.cv, axis=0)
    tw_s = jnp.concatenate([tw_s * scale] * plan.cv, axis=0)

    for load in loads[2:]:
        load.wait()
    wait(recv_sem, 0, r_a)

    data = r_a[...].astype(F32).reshape(half, 128).astype(BF16)
    total = jnp.dot(high[...], data, preferred_element_type=F32)
    total += jnp.dot(low[...], data, preferred_element_type=F32)
    s_b[...] = total.reshape(plan.xg, plan.q, 128)
    across(1, s_b, r_b)

    wait(recv_sem, 6, r_p)
    base = jnp.broadcast_to(r_p[...], (devices, 4, 128)).reshape(devices * 4, 128)
    base = base + (lax.broadcasted_iota(jnp.int32, base.shape, 0) & 3)
    in_tile = lax.broadcasted_iota(jnp.int32, base.shape, 1)
    for h in range(plan.th):
        m = base + 4 * h
        at = pl.ds(h * devices * 4, devices * 4)
        for g in range(plan.xg):
            lanes = pl.ds(g * 128, 128)
            tc, ts = circle((m * (in_tile + g * plan.xl)) & (SG - 1), SG)
            tch[at, lanes], tcl[at, lanes] = split(tc)
            tsh[at, lanes], tsl[at, lanes] = split(ts)

    wait(recv_sem, 1, r_b)

    a = jnp.concatenate([r_b[g] for g in range(plan.xg)], axis=1)
    a = a * tw_c + swapped(a) * tw_s
    a_h, a_l = split(a)
    w_h, w_l = split(swapped(a))
    grid = nt(tch[...], jnp.concatenate([a_h, a_l], axis=0))
    grid += nt(tsh[...], jnp.concatenate([w_h, w_l], axis=0))
    grid = grid[:, : plan.q] + grid[:, plan.q :]
    grid += nt(tcl[...], a_h) + nt(tsl[...], w_h)
    s_c[...] = to_slots(plan, grid).astype(BF16)
    send(2, s_c, r_c)

    cu = u_fine[...] // OVER
    shift = (KS - 1) / 2.0 + (u_fine[...] % OVER).astype(F32) / OVER
    part = plan.xg * plan.res
    for t in range(4 * plan.th):
        row = lax.broadcasted_iota(jnp.int32, (part, u_fine.shape[1]), 0)
        offset = row + plan.nb * t - cu
        distance = (offset.astype(F32) - shift) / 0.6
        weight = jnp.exp(-0.5 * distance * distance)
        weight = jnp.where((offset >= 0) & (offset < KS), weight, 0.0)
        wu[pl.ds(t * part, part), :] = weight.astype(BF16)

    span = plan.th * plan.vg * 4
    shape = (plan.cv * span, v_fine.shape[1])
    row = lax.broadcasted_iota(jnp.int32, shape, 0)
    v = lax.rem(lax.div(row, span), plan.v2) + lax.rem(row >> 2, plan.vg) * plan.v2
    offset = v - v_fine[...] // OVER
    shift = (KS - 1) / 2.0 + (v_fine[...] % OVER).astype(F32) / OVER
    distance = (offset.astype(F32) - shift) / 0.6
    wv = jnp.exp(-0.5 * distance * distance)
    wv = jnp.where((offset >= 0) & (offset < KS), wv, 0.0)

    wait(recv_sem, 2, r_c)

    cells = from_slots(plan, r_c[...], plan.xg)
    cells = cells.reshape(plan.xg, span, plan.q)
    cells = jnp.concatenate([cells[g] for g in range(plan.xg)], axis=1).T
    cells = cells.reshape(plan.xg, plan.cv, plan.res, span)
    cells = [cells[:, i].reshape(part, span) for i in range(plan.cv)]
    cells = jnp.concatenate(cells, axis=1)
    place_in = lax.rem(lax.broadcasted_iota(jnp.int32, cells.shape, 1), span)
    time = lax.div(place_in, plan.vg * 4) * 4 + (place_in & 3)
    times = range(4 * plan.th)
    cells = jnp.concatenate([jnp.where(time == t, cells, 0.0) for t in times], axis=0)
    along = tn(cells.astype(BF16), wu[...]) * wv
    middle = shape[0] // 2
    live = lax.broadcasted_iota(jnp.int32, (1, shape[1]), 1) < count[...]
    real = jnp.where(live, observed[0] - jnp.sum(along[:middle], axis=0, keepdims=True), 0.0)
    imag = jnp.where(live, observed[1] - jnp.sum(along[middle:], axis=0, keepdims=True), 0.0)
    res[0] = real
    res[1] = imag
    kept = pltpu.make_async_copy(res, res_out, load_sem.at[0])
    kept.start()
    row = lax.broadcasted_iota(jnp.int32, shape, 0)
    spread = (wv * jnp.where(row < middle, real, imag)).astype(BF16)
    both = nt(wu[...], spread)
    regrid = both[:part]
    for t in times[1:]:
        regrid = jnp.where(time == t, both[t * part : (t + 1) * part], regrid)
    regrid = [regrid[:, i * span : (i + 1) * span] for i in range(plan.cv)]
    regrid = [one.reshape(plan.xg, 1, plan.res, span) for one in regrid]
    regrid = jnp.concatenate(regrid, axis=1).reshape(plan.xg * plan.q, span).T
    regrid = [
        to_rows(plan, regrid[:, g * plan.q : (g + 1) * plan.q]) for g in range(plan.xg)
    ]
    regrid = jnp.concatenate(regrid, axis=0)
    s_d[...] = regrid.reshape(devices, 4, plan.th * plan.q).astype(BF16)
    send(3, s_d, r_d)
    wait(recv_sem, 3, r_d)

    cells = from_slots(plan, r_d[...], 1).astype(BF16)
    a = tn(cells, tch[...]) - swapped(tn(cells, tsh[...]))
    a = a * tw_c - swapped(a) * tw_s
    for g in range(plan.xg):
        s_e[g] = a[:, g * 128 : (g + 1) * 128].astype(BF16)
    across(4, s_e, r_e)
    wait(recv_sem, 4, r_e)

    data = r_e[...].reshape(plan.xg * plan.q, 128)
    total = jnp.dot(back[...], data, preferred_element_type=F32)
    s_f[...] = total.reshape(devices, 8, 128).astype(BF16)
    send(5, s_f, r_f, local=True)
    own = pltpu.make_async_copy(s_f.at[me], r_f.at[me], load_sem.at[1])
    own.start()
    wait(recv_sem, 5, r_f)
    own.wait()
    kept.wait()

    for phase, sent in enumerate((r_a, r_b, r_c, r_d, r_e, r_f, r_p)):
        wait(send_sem, phase, sent)


def finish(plan, residual, got, res_out, image_out, image, slots):
    res_out[...] = residual[...]
    tiles = image_out.shape[2] // 128
    per = 128 // plan.xl
    lane = lax.broadcasted_iota(jnp.int32, (plan.vg, 128), 1)
    slots[...] = got[...].astype(F32).reshape(plan.devices * 8, 128)
    for c in range(2):
        for k in range(plan.rl):
            for v in range(plan.v2):
                for g in range(0, plan.xg, per):
                    value = slots[rows(plan, c, k, v, g), :]
                    for n in range(1, per):
                        more = pltpu.roll(slots[rows(plan, c, k, v, g + n), :], n * plan.xl, 1)
                        value = jnp.where(lane < n * plan.xl, value, more)
                    tile = (k * SG + g * plan.xl) // 128
                    image[c, tile, pl.ds(v, plan.vg, stride=plan.v2), :] = value
    for k in range(tiles):
        image_out[:, :, k * 128 : (k + 1) * 128] = image[:, k]


def shards(facet_data, subgrid_pos, vis_counts, vis_u_fine, vis_v_fine, vis_observed):
    nsub = lax.axis_size("sub")
    devices = lax.axis_size("facet") * nsub
    plan = Plan(devices, nsub, facet_data.shape[1], facet_data.shape[2])
    slots = vis_u_fine.shape[1]

    table = block_transform(plan)
    high = table.astype(BF16)
    low = (table - high.astype(np.float32)).astype(BF16)

    wide = pltpu.VMEM((plan.xg, plan.q, 128), F32)
    narrow = pltpu.VMEM((plan.xg, plan.q, 128), BF16)
    tile = pltpu.VMEM((devices, 8, 128), BF16)
    cell = pltpu.VMEM((devices, 4, plan.th * plan.q), BF16)
    turn = pltpu.VMEM((plan.rows, plan.x), BF16)
    rows_v, columns = facet_data.shape[1:]
    operands = (
        facet_data, subgrid_pos.reshape(1, 1), vis_u_fine, vis_v_fine, vis_observed,
        vis_counts.reshape(1, 1), jnp.asarray(high), jnp.asarray(low), jnp.asarray(high.T),
    )
    residual, got = pl.pallas_call(
        functools.partial(kernel, plan),
        out_shape=(
            jax.ShapeDtypeStruct(vis_observed.shape, F32),
            jax.ShapeDtypeStruct((devices, 8, 128), BF16),
        ),
        in_specs=[pl.BlockSpec(memory_space=pltpu.HBM)] * 9,
        out_specs=(pl.BlockSpec(memory_space=pltpu.HBM),) * 2,
        scratch_shapes=[
            pltpu.VMEM((2, columns // 128, rows_v, 128), F32),
            pltpu.VMEM((devices * 8, 128), F32),
            tile, tile,
            pltpu.VMEM((1, 128), jnp.int32),
            pltpu.VMEM((devices, 1, 128), jnp.int32),
            wide, wide, cell, cell, cell, cell, narrow, narrow, tile,
            pltpu.VMEM(vis_observed.shape, F32),
            pltpu.VMEM((4 * plan.th * plan.nb, slots), BF16),
            turn, turn, turn, turn,
            pltpu.SemaphoreType.DMA((7,)),
            pltpu.SemaphoreType.DMA((7,)),
            pltpu.SemaphoreType.DMA((9,)),
        ]
        + [pltpu.VMEM(one.shape, one.dtype) for one in operands],
        compiler_params=pltpu.CompilerParams(
            collective_id=0, has_side_effects=True, vmem_limit_bytes=64 * 1024 * 1024 - 65536
        ),
    )(*operands)
    return pl.pallas_call(
        functools.partial(finish, plan),
        out_shape=(
            jax.ShapeDtypeStruct(vis_observed.shape, F32),
            jax.ShapeDtypeStruct(facet_data.shape, F32),
        ),
        in_specs=[pl.BlockSpec(memory_space=pltpu.VMEM)] * 2,
        out_specs=(pl.BlockSpec(memory_space=pltpu.VMEM),) * 2,
        scratch_shapes=[
            pltpu.VMEM((2, columns // 128, rows_v, 128), F32),
            pltpu.VMEM((devices * 8, 128), F32),
        ],
        compiler_params=pltpu.CompilerParams(vmem_limit_bytes=64 * 1024 * 1024 - 65536),
    )(residual, got)


def solution(mesh):
    return jax.shard_map(
        shards,
        mesh=mesh,
        in_specs=(
            P(None, None, ("facet", "sub")),
            P(("facet", "sub")),
            P(("facet", "sub")),
            P(("facet", "sub"), None),
            P(("facet", "sub"), None),
            P(None, ("facet", "sub"), None),
        ),
        out_specs=(P(None, ("facet", "sub"), None), P(None, None, ("facet", "sub"))),
        check_vma=False,
    )
```
